256 devices in a mesh: dp: 16 (over x, y_hi, core), tensor: 16 (over z, y_lo).
Axes of the slice: x: 4, y: 4 (y_hi: 2, y_lo: 2; y = y_hi * 2 + y_lo), z: 8, core: 2. Of those that a mesh axis runs over, the one named last changes fastest.
Arguments:
- decoder_input: bfloat16 [2, 512, 16384], P(None, 'tensor', 'dp')
- norm_multiplier: bfloat16 [16384], P('dp'), may hold values from 0.5 to 2
- query_weight: bfloat16 [16384, 16384], P('dp', 'tensor'), may hold values from -0.046875 to 0.046875
- key_weight: bfloat16 [16384, 1024], P('dp', 'tensor'), may hold values from -0.046875 to 0.046875
- value_weight: bfloat16 [16384, 1024], P('dp', 'tensor'), may hold values from -0.046875 to 0.046875
- output_weight: bfloat16 [16384, 16384], P('tensor', 'dp'), may hold values from -0.046875 to 0.046875
- key_value_cache: bfloat16 [512, 128, 2, 1024], P(('dp', 'tensor'))
- lengths: int32 [512], P(('dp', 'tensor')), may hold values from 16 to 128, as said below
- training_input: bfloat16 [2048, 16384], P('dp', 'tensor'), may hold values from -6 to 6
- query_gradient: bfloat16 [2048, 16384], P('dp', 'tensor'), may hold values from -6 to 6
- attention_mixed: bfloat16 [2048, 16384], P('dp', 'tensor'), may hold values from -6 to 6
- output_gradient: bfloat16 [2048, 16384], P('dp', 'tensor'), may hold values from -6 to 6
- rewards: int32 [32], replicated, may hold values from 0 to 4
- adapter_down: float32 [2, 64, 16384], P(None, None, 'tensor'), may hold values from -6 to 6
- adapter_up: float32 [2, 64, 16384], P(None, None, 'tensor'), may hold values from -6 to 6
- down_mean_moment: bfloat16 [2, 64, 16384], P(None, None, 'tensor'), may hold values from -5 to 5
- up_mean_moment: bfloat16 [2, 64, 16384], P(None, None, 'tensor'), may hold values from -5 to 5
- down_variance_moment: bfloat16 [2, 64, 16384], P(None, None, 'tensor'), may hold values from 0.031982422 to 0.31835938
- up_variance_moment: bfloat16 [2, 64, 16384], P(None, None, 'tensor'), may hold values from 0.031982422 to 0.31835938
Outputs:
- attn_out: bfloat16 [2, 512, 16384], P(None, 'tensor', 'dp')
- refreshed_down: float32 [2, 64, 16384], P(None, None, 'tensor')
- refreshed_up: float32 [2, 64, 16384], P(None, None, 'tensor')
- refreshed_down_mean: bfloat16 [2, 64, 16384], P(None, None, 'tensor')
- refreshed_up_mean: bfloat16 [2, 64, 16384], P(None, None, 'tensor')
- refreshed_down_variance: bfloat16 [2, 64, 16384], P(None, None, 'tensor')
- refreshed_up_variance: bfloat16 [2, 64, 16384], P(None, None, 'tensor')
The draws below stay inside these ranges and needn't reach their ends.
Inputs may be any that keep to these rules, and one draw needn't show every extreme that they name: `lengths`: some row has exactly 128 valid positions.
All inputs are finite; a program needn't handle non-finite values.
Results may differ from the reference program's by a relative error of at most 0.035.
Values may be sent and summed in bfloat16 or wider, within the bound.
No kernel may reach another device: no remote copies, remote signals or barrier semaphores. Data moves between devices by JAX's collectives and lax.ppermute only.
A program may use at most 64 MiB of HBM per device.

```python
import math
import jax
import jax.numpy as jnp
from jax import lax

MODEL_WIDTH = 16384
QUERY_HEADS = 128
HEAD_WIDTH = 128
KEY_VALUE_HEADS = 8
FACTOR_RANK = 64
STEPS = 2
CACHE_SLOTS = 128
SEQLEN = 64
GROUP = 8
HQ = 16384
KVW = 1024
ROWS = 512
LTOK = 2048
NSEQ = 32
N_DP = 16
N_TENSOR = 16


def draw_decoder_input(key, part):
    key = jax.random.fold_in(key, 11)
    key_base, key_rows, key_cols = jax.random.split(key, 3)
    shape = (STEPS, ROWS, MODEL_WIDTH)
    base = jax.random.normal(key_base, shape, jnp.float32)
    row_scale = jnp.exp(jax.random.uniform(key_rows, (STEPS, ROWS, 1), jnp.float32, 0.0, math.log(10.0)))
    ramp = jnp.exp(math.log(3.0) * jnp.arange(MODEL_WIDTH, dtype=jnp.float32) / MODEL_WIDTH)
    col_scale = ramp * jnp.exp(jax.random.uniform(key_cols, (MODEL_WIDTH,), jnp.float32, 0.0, math.log(10.0)))
    return (0.05 * base * row_scale * col_scale).astype(jnp.bfloat16)


def draw_key_value_cache(key, part):
    key = jax.random.fold_in(key, 23)
    key_base = jax.random.fold_in(key, 0)
    shape = (ROWS, CACHE_SLOTS, 2, KVW)
    base = jax.random.normal(key_base, shape, jnp.float32)
    return base.astype(jnp.bfloat16)


def draw_lengths(key, part):
    key = jax.random.fold_in(key, 37)
    key_len, key_spot = jax.random.split(key, 2)
    lowest = max(2, CACHE_SLOTS // 8)
    drawn = jax.random.randint(key_len, (ROWS,), lowest, CACHE_SLOTS + 1, jnp.int32)
    spot = jax.random.randint(key_spot, (), 0, ROWS, jnp.int32)
    return jnp.where(jnp.arange(ROWS, dtype=jnp.int32) == spot, CACHE_SLOTS, drawn).astype(jnp.int32)


def place_ends(result, rng, low, high):
    spot = [jax.random.randint(jax.random.fold_in(rng, axis), (), 0, length) for axis, length in enumerate(result.shape)]
    main_axis = result.shape.index(max(result.shape))
    next_to = spot[:main_axis] + [(spot[main_axis] + 1) % result.shape[main_axis]] + spot[main_axis + 1:]
    return result.at[tuple(spot)].set(low).at[tuple(next_to)].set(high)


def shard_levels(own_key, dims, cuts, smallest, largest):
    loudness, own = 1.0, jax.random.fold_in(own_key, 6)
    for position, shards_of in cuts:
        heights = jnp.exp(jax.random.uniform(jax.random.fold_in(own, position), (shards_of,), jnp.float32, smallest / len(cuts), largest / len(cuts)))
        loudness = loudness * jnp.repeat(heights, dims[position] // shards_of).reshape([-1 if axis == position else 1 for axis in range(len(dims))])
    return loudness


def scatter_about(rng, shape, spread, reach, cuts=(), held_as=jnp.bfloat16):
    values = spread * jax.random.normal(rng, shape, jnp.float32)
    if cuts:
        values = values * shard_levels(rng, shape, cuts, -0.22, 0.18)
    return jnp.clip(values, -reach, reach).astype(held_as)


def setup_inputs(seed: int = 0) -> dict:
    seeds = jax.random.split(jax.random.key(seed), 20)
    decoder_input = draw_decoder_input(jax.random.fold_in(seeds[19], 71), 0)
    norm_multiplier = jnp.clip(jnp.exp(math.log(2.0) - 1.3862944 * jax.random.uniform(seeds[1], (MODEL_WIDTH,), jnp.float32) ** shard_levels(seeds[1], (MODEL_WIDTH,), ((0, 16),), -0.2, 0.2)), 0.5, 2.0).astype(jnp.bfloat16)
    query_weight = scatter_about(seeds[2], (MODEL_WIDTH, HQ), MODEL_WIDTH ** -0.5, 0.046875, ((0, 16), (1, 16)))
    key_weight = scatter_about(seeds[3], (MODEL_WIDTH, KVW), MODEL_WIDTH ** -0.5, 0.046875, ((0, 16), (1, 16)))
    value_weight = scatter_about(seeds[4], (MODEL_WIDTH, KVW), MODEL_WIDTH ** -0.5, 0.046875, ((0, 16), (1, 16)))
    output_weight = scatter_about(seeds[5], (HQ, MODEL_WIDTH), HQ ** -0.5, 0.046875, ((0, 16), (1, 16)))
    key_value_cache = draw_key_value_cache(jax.random.fold_in(seeds[19], 71), 0)
    lengths = draw_lengths(jax.random.fold_in(seeds[19], 71), 0)
    training_input = scatter_about(seeds[8], (LTOK, MODEL_WIDTH), 1.0, 6.0, ((0, 16), (1, 16)))
    query_gradient = scatter_about(seeds[9], (LTOK, HQ), 1.0, 6.0, ((0, 16), (1, 16)))
    attention_mixed = scatter_about(seeds[10], (LTOK, HQ), 1.0, 6.0, ((0, 16), (1, 16)))
    output_gradient = scatter_about(seeds[11], (LTOK, MODEL_WIDTH), 1.0, 6.0, ((0, 16), (1, 16)))
    rewards = place_ends(jax.random.randint(seeds[12], (NSEQ,), 0, 5), jax.random.fold_in(seeds[12], 1), 0, 4).astype(jnp.int32)
    adapter_down = scatter_about(seeds[13], (2, FACTOR_RANK, MODEL_WIDTH), 1.0, 6.0, ((2, 16),), jnp.float32)
    adapter_up = scatter_about(seeds[14], (2, FACTOR_RANK, MODEL_WIDTH), 1.0, 6.0, ((2, 16),), jnp.float32)
    down_mean_moment = scatter_about(seeds[15], (2, FACTOR_RANK, MODEL_WIDTH), (0.15 * (LTOK // FACTOR_RANK) ** 0.5), 5.0, ((2, 16),))
    up_mean_moment = scatter_about(seeds[16], (2, FACTOR_RANK, MODEL_WIDTH), (0.15 * (LTOK // FACTOR_RANK) ** 0.5), 5.0, ((2, 16),))
    down_variance_moment = jnp.clip(jnp.exp(math.log(0.31835938) - 2.2979944 * jax.random.uniform(seeds[17], (2, FACTOR_RANK, MODEL_WIDTH), jnp.float32) ** shard_levels(seeds[17], (2, FACTOR_RANK, MODEL_WIDTH), ((2, 16),), -0.2, 0.2)), 0.031982422, 0.31835938).astype(jnp.bfloat16)
    up_variance_moment = jnp.clip(jnp.exp(math.log(0.31835938) - 2.2979944 * jax.random.uniform(seeds[18], (2, FACTOR_RANK, MODEL_WIDTH), jnp.float32) ** shard_levels(seeds[18], (2, FACTOR_RANK, MODEL_WIDTH), ((2, 16),), -0.2, 0.2)), 0.031982422, 0.31835938).astype(jnp.bfloat16)
    return dict(decoder_input=decoder_input, norm_multiplier=norm_multiplier, query_weight=query_weight, key_weight=key_weight, value_weight=value_weight, output_weight=output_weight, key_value_cache=key_value_cache, lengths=lengths, training_input=training_input, query_gradient=query_gradient, attention_mixed=attention_mixed, output_gradient=output_gradient, rewards=rewards, adapter_down=adapter_down, adapter_up=adapter_up, down_mean_moment=down_mean_moment, up_mean_moment=up_mean_moment, down_variance_moment=down_variance_moment, up_variance_moment=up_variance_moment)


BETA_ONE = 0.9
BETA_TWO = 0.999
BIAS_ONE = 0.271
BIAS_TWO = 0.002997001
LEARN_RATE = 0.3
ADAM_EPS = 1e-08
NORM_EPS = 1e-05
NEG_FILL = -1e+30

def apply_adam_rule(parameter, gradient, first_moment, second_moment):
    moment_one = BETA_ONE * first_moment.astype(jnp.float32) + (1.0 - BETA_ONE) * gradient
    moment_two = BETA_TWO * second_moment.astype(jnp.float32) + (1.0 - BETA_TWO) * gradient * gradient
    change = moment_one / BIAS_ONE / (jnp.sqrt(moment_two / BIAS_TWO) + ADAM_EPS)
    return (parameter - LEARN_RATE * change, moment_one.astype(jnp.bfloat16), moment_two.astype(jnp.bfloat16))

def leading_contraction(lhs_array, rhs_array):
    return lax.dot_general(lhs_array, rhs_array, (((0,), (0,)), ((), ())), preferred_element_type=jnp.float32)

def contract_last(lhs_array, rhs_array):
    return lax.dot_general(lhs_array, rhs_array, (((1,), (1,)), ((), ())), preferred_element_type=jnp.float32)

def combine_weight(weight_matrix, reduced_down, reduced_up, adapter_factor, pieces):
    span = weight_matrix.shape[0] // pieces

    def merge_block(number):
        begin = (number * span).astype(jnp.int32)
        block_of_rows = lax.dynamic_slice_in_dim(weight_matrix, begin, span, 0)
        down_cols = lax.dynamic_slice_in_dim(reduced_down, begin, span, 1)
        weight_change = leading_contraction(down_cols, reduced_up)
        return (block_of_rows.astype(jnp.float32) + adapter_factor * weight_change).astype(jnp.bfloat16)
    merged = lax.map(merge_block, jnp.arange(pieces, dtype=jnp.int32))
    return merged.reshape(weight_matrix.shape)

def blocked_product(lhs_array, rhs_array, pieces):
    span = lhs_array.shape[1] // pieces

    def accumulate(number, carried):
        begin = (number * span).astype(jnp.int32)
        lhs_cols = lax.dynamic_slice_in_dim(lhs_array, begin, span, 1)
        rhs_rows = lax.dynamic_slice_in_dim(rhs_array, begin, span, 0)
        return carried + jnp.dot(lhs_cols, rhs_rows, preferred_element_type=jnp.float32)
    start_value = jnp.zeros((lhs_array.shape[0], rhs_array.shape[1]), jnp.float32)
    return lax.fori_loop(0, pieces, accumulate, start_value)

def attend_rows(query_rows, cache_of_keys, cache_of_values, valid, latest_keys, latest_values):
    count_of_rows = query_rows.shape[0]
    scale_att = 1.0 / math.sqrt(HEAD_WIDTH)
    query_groups = query_rows.astype(jnp.float32).reshape(count_of_rows, KEY_VALUE_HEADS, QUERY_HEADS // KEY_VALUE_HEADS, HEAD_WIDTH)
    cache_scores = jnp.einsum('rkgd,rpkd->rkgp', query_groups, cache_of_keys.astype(jnp.float32)) * scale_att
    cache_scores = jnp.where(valid[:, None, None, :], cache_scores, NEG_FILL)
    stacked_keys = jnp.stack(latest_keys, axis=1).reshape(count_of_rows, len(latest_keys), KEY_VALUE_HEADS, HEAD_WIDTH)
    stacked_values = jnp.stack(latest_values, axis=1).reshape(count_of_rows, len(latest_values), KEY_VALUE_HEADS, HEAD_WIDTH)
    fresh_scores = jnp.einsum('rkgd,rpkd->rkgp', query_groups, stacked_keys.astype(jnp.float32)) * scale_att
    scores = jnp.concatenate([cache_scores, fresh_scores], axis=-1)
    row_top = lax.optimization_barrier(jnp.max(scores, axis=-1, keepdims=True))
    exponent = jnp.exp(scores - row_top)
    attention_weights = (exponent / lax.optimization_barrier(jnp.sum(exponent, axis=-1, keepdims=True))).astype(jnp.bfloat16)
    cache_part = jnp.einsum('rkgp,rpkd->rkgd', attention_weights[..., :CACHE_SLOTS].astype(jnp.float32), cache_of_values.astype(jnp.float32))
    fresh_part = jnp.einsum('rkgp,rpkd->rkgd', attention_weights[..., CACHE_SLOTS:].astype(jnp.float32), stacked_values.astype(jnp.float32))
    return (cache_part + fresh_part).reshape(count_of_rows, QUERY_HEADS * HEAD_WIDTH).astype(jnp.bfloat16)

def reference(decoder_input, norm_multiplier, query_weight, key_weight, value_weight, output_weight, key_value_cache, lengths, training_input, query_gradient, attention_mixed, output_gradient, rewards, adapter_down, adapter_up, down_mean_moment, up_mean_moment, down_variance_moment, up_variance_moment):
    adapter_factor = 1.0 / math.sqrt(MODEL_WIDTH * FACTOR_RANK)
    grouped = rewards.astype(jnp.float32).reshape(-1, GROUP)
    advantage = (grouped - lax.optimization_barrier(jnp.mean(grouped, axis=1, keepdims=True))).reshape(-1)
    token_weight = jnp.repeat(advantage, SEQLEN)
    query_cotangent = (token_weight[:, None] * query_gradient.astype(jnp.float32)).astype(jnp.bfloat16)
    output_cotangent = (token_weight[:, None] * output_gradient.astype(jnp.float32)).astype(jnp.bfloat16)
    down_reduced = adapter_down.astype(jnp.bfloat16)
    up_reduced = adapter_up.astype(jnp.bfloat16)
    decoder_query = contract_last(training_input, down_reduced[0]).astype(jnp.bfloat16)
    decoder_output = contract_last(attention_mixed, down_reduced[1]).astype(jnp.bfloat16)
    query_backward = contract_last(query_cotangent, up_reduced[0]).astype(jnp.bfloat16)
    output_backward = contract_last(output_cotangent, up_reduced[1]).astype(jnp.bfloat16)
    down_gradient = adapter_factor * jnp.stack([leading_contraction(query_backward, training_input), leading_contraction(output_backward, attention_mixed)])
    up_gradient = adapter_factor * jnp.stack([leading_contraction(decoder_query, query_cotangent), leading_contraction(decoder_output, output_cotangent)])
    refreshed_down, refreshed_down_mean, refreshed_down_variance = apply_adam_rule(adapter_down, down_gradient, down_mean_moment, down_variance_moment)
    refreshed_up, refreshed_up_mean, refreshed_up_variance = apply_adam_rule(adapter_up, up_gradient, up_mean_moment, up_variance_moment)
    combined_down = refreshed_down.astype(jnp.bfloat16)
    combined_up = refreshed_up.astype(jnp.bfloat16)
    query_combined = combine_weight(query_weight, combined_down[0], combined_up[0], adapter_factor, N_DP)
    output_combined = combine_weight(output_weight, combined_down[1], combined_up[1], adapter_factor, N_DP)
    weight_all = jnp.concatenate([query_combined, key_weight, value_weight], axis=1)
    count_of_rows = key_value_cache.shape[0]
    cache_of_keys = key_value_cache[:, :, 0, :].reshape(count_of_rows, CACHE_SLOTS, KEY_VALUE_HEADS, HEAD_WIDTH)
    cache_of_values = key_value_cache[:, :, 1, :].reshape(count_of_rows, CACHE_SLOTS, KEY_VALUE_HEADS, HEAD_WIDTH)
    valid = jnp.arange(CACHE_SLOTS, dtype=jnp.int32)[None, :] < lengths[:, None]
    latest_keys = []
    latest_values = []
    results = []
    for decode_step in range(STEPS):
        current = decoder_input[decode_step].astype(jnp.float32)
        mean_square = lax.optimization_barrier(jnp.mean(current * current, axis=1, keepdims=True))
        normed = (current * lax.rsqrt(mean_square + NORM_EPS) * norm_multiplier.astype(jnp.float32)).astype(jnp.bfloat16)
        projection_result = blocked_product(normed, weight_all, N_DP).astype(jnp.bfloat16)
        query_rows = projection_result[:, :QUERY_HEADS * HEAD_WIDTH]
        latest_keys.append(projection_result[:, QUERY_HEADS * HEAD_WIDTH:QUERY_HEADS * HEAD_WIDTH + KEY_VALUE_HEADS * HEAD_WIDTH])
        latest_values.append(projection_result[:, QUERY_HEADS * HEAD_WIDTH + KEY_VALUE_HEADS * HEAD_WIDTH:])
        attended = attend_rows(query_rows, cache_of_keys, cache_of_values, valid, latest_keys, latest_values)
        results.append(blocked_product(attended, output_combined, N_TENSOR).astype(jnp.bfloat16))
    attn_out = jnp.stack(results)
    return (attn_out, refreshed_down, refreshed_up, refreshed_down_mean, refreshed_up_mean, refreshed_down_variance, refreshed_up_variance)
```

```python
import math

import jax
import jax.numpy as jnp
from jax import lax
from jax.sharding import PartitionSpec as P

MODEL_WIDTH = 16384
QUERY_HEADS = 128
HEAD_WIDTH = 128
KEY_VALUE_HEADS = 8
FACTOR_RANK = 64
STEPS = 2
CACHE_SLOTS = 128
SEQLEN = 64
GROUP = 8


BETA_ONE = 0.9
BETA_TWO = 0.999
BIAS_ONE = 0.271
BIAS_TWO = 0.002997001
LEARN_RATE = 0.3
ADAM_EPS = 1e-08
NORM_EPS = 1e-05
NEG_FILL = -1e30


def apply_adam_rule(parameter, gradient, first_moment, second_moment):
    moment_one = BETA_ONE * first_moment.astype(jnp.float32) + (1.0 - BETA_ONE) * gradient
    moment_two = (
        BETA_TWO * second_moment.astype(jnp.float32) + (1.0 - BETA_TWO) * gradient * gradient
    )
    change = moment_one / BIAS_ONE / (jnp.sqrt(moment_two / BIAS_TWO) + ADAM_EPS)
    return (
        parameter - LEARN_RATE * change,
        moment_one.astype(jnp.bfloat16),
        moment_two.astype(jnp.bfloat16),
    )


def leading_contraction(lhs_array, rhs_array):
    return lax.dot_general(
        lhs_array, rhs_array, (((0,), (0,)), ((), ())), preferred_element_type=jnp.float32
    )


def contract_last(lhs_array, rhs_array):
    return lax.dot_general(
        lhs_array, rhs_array, (((1,), (1,)), ((), ())), preferred_element_type=jnp.float32
    )


def attend_rows(query_rows, cache_of_keys, cache_of_values, valid, latest_keys, latest_values):
    scale_att = 1.0 / math.sqrt(HEAD_WIDTH)
    cache_scores = (
        jnp.einsum("rkgd,rpkd->rkgp", query_rows, cache_of_keys, preferred_element_type=jnp.float32)
        * scale_att
    )
    cache_scores = jnp.where(valid[:, None, None, :], cache_scores, NEG_FILL)
    fresh_scores = (
        jnp.einsum("rkgd,rpkd->rkgp", query_rows, latest_keys, preferred_element_type=jnp.float32)
        * scale_att
    )
    group = QUERY_HEADS // KEY_VALUE_HEADS
    query_step = jnp.arange(STEPS * group, dtype=jnp.int32) // group
    seen = jnp.arange(STEPS, dtype=jnp.int32)[None, :] <= query_step[:, None]
    fresh_scores = jnp.where(seen[None, None], fresh_scores, NEG_FILL)
    scores = jnp.concatenate([cache_scores, fresh_scores], axis=-1)
    row_top = jnp.max(scores, axis=-1, keepdims=True)
    exponent = jnp.exp(scores - row_top)
    attention_weights = (exponent / jnp.sum(exponent, axis=-1, keepdims=True)).astype(jnp.bfloat16)
    cache_part = jnp.einsum(
        "rkgp,rpkd->rkgd",
        attention_weights[..., :CACHE_SLOTS],
        cache_of_values,
        preferred_element_type=jnp.float32,
    )
    fresh_part = jnp.einsum(
        "rkgp,rpkd->rkgd",
        attention_weights[..., CACHE_SLOTS:],
        latest_values,
        preferred_element_type=jnp.float32,
    )
    return (cache_part + fresh_part).astype(jnp.bfloat16)


def hop_dp(array, target):
    return lax.ppermute(array, "dp", [(s, target(s)) for s in range(16)])


def hop_tensor(array, target):
    return lax.ppermute(array, "tensor", [(s, target(s)) for s in range(16)])


def other_core(array):
    return hop_dp(array, lambda s: s ^ 1)


def other_half(array):
    return hop_dp(array, lambda s: s ^ 2)


def x_up(array):
    return hop_dp(array, lambda s: (s + 4) % 16)


def x_down(array):
    return hop_dp(array, lambda s: (s - 4) % 16)


def other_y(array):
    return hop_tensor(array, lambda s: s ^ 1)


def z_up(array):
    return hop_tensor(array, lambda s: (s + 2) % 16)


def z_down(array):
    return hop_tensor(array, lambda s: (s - 2) % 16)


def pick(array, index, axis=0):
    return lax.dynamic_index_in_dim(array, index, axis, keepdims=False)


def add_up(*arrays):
    total = arrays[0].astype(jnp.float32)
    for array in arrays[1:]:
        total = total + array.astype(jnp.float32)
    return total


def cores_summed(pair, keep):
    kept, sent = pick(pair, keep, 1), pick(pair, 1 - keep, 1)
    return add_up(kept, other_core(sent)).astype(pair.dtype)


def scatter_xy(block, half):
    kind = block(0).dtype
    far, ahead, behind = block(2), block(1), block(3)
    low, high = x_up(far[0]), x_down(far[1])
    ahead = jnp.stack([add_up(ahead[0], low).astype(kind), ahead[1]])
    behind = jnp.stack([behind[0], add_up(behind[1], high).astype(kind)])
    total = add_up(block(0), x_up(ahead), x_down(behind))
    kept, sent = pick(total, half), pick(total, 1 - half).astype(kind)
    return add_up(kept, other_half(sent))


def in_order(own, other, position):
    first = jnp.where(position == 0, own, other)
    second = jnp.where(position == 0, other, own)
    return first, second


def gather_xy(array, half):
    own = jnp.stack(in_order(array, other_half(array), half))
    behind, ahead = x_up(own), x_down(own)
    far = jnp.stack([x_up(behind[0]), x_down(ahead[1])])
    return jnp.stack([own, ahead, far, behind])


def on_device(
    decoder_input,
    norm_multiplier,
    query_weight,
    key_weight,
    value_weight,
    output_weight,
    key_value_cache,
    lengths,
    training_input,
    query_gradient,
    attention_mixed,
    output_gradient,
    rewards,
    adapter_down,
    adapter_up,
    down_mean_moment,
    up_mean_moment,
    down_variance_moment,
    up_variance_moment,
):
    adapter_factor = 1.0 / math.sqrt(MODEL_WIDTH * FACTOR_RANK)
    dp_index = lax.axis_index("dp")
    tensor_index = lax.axis_index("tensor")
    at_x, half, core = dp_index // 4, (dp_index // 2) % 2, dp_index % 2
    at_z, at_y = tensor_index // 2, tensor_index % 2
    core_differs = core ^ at_y
    bf16 = jnp.bfloat16

    rows = decoder_input.reshape(STEPS * decoder_input.shape[1], -1)
    own = jnp.stack([rows, other_y(rows)])
    gathered = [own]
    up, down = own, own
    for _ in range(3):
        up, down = z_up(up), z_down(down)
        gathered += [up, down]
    gathered.append(jnp.stack([z_up(up[0]), z_down(down[1])]))
    distance = (0, 7, 1, 6, 2, 5, 3, 4)
    slot_of = jnp.array([distance.index(d) for d in range(8)], jnp.int32)

    local_seqs = training_input.shape[0] // SEQLEN
    grouped = rewards.astype(jnp.float32).reshape(-1, GROUP)
    advantage = (grouped - jnp.mean(grouped, axis=1, keepdims=True)).reshape(-1)
    own_advantage = lax.dynamic_slice_in_dim(advantage, dp_index * local_seqs, local_seqs, 0)
    token_weight = jnp.repeat(own_advantage, SEQLEN)
    query_cotangent = (token_weight[:, None] * query_gradient.astype(jnp.float32)).astype(bf16)
    output_cotangent = (token_weight[:, None] * output_gradient.astype(jnp.float32)).astype(bf16)
    down_reduced = adapter_down.astype(bf16)
    up_reduced = adapter_up.astype(bf16)
    ranks = jnp.concatenate(
        [
            contract_last(training_input, down_reduced[0]),
            contract_last(attention_mixed, down_reduced[1]),
            contract_last(query_cotangent, up_reduced[0]),
            contract_last(output_cotangent, up_reduced[1]),
        ],
        axis=1,
    ).astype(bf16)
    for bits in ((1, 2, 3), (4, 8, 12)):
        others = [hop_tensor(ranks, lambda s, b=b: s ^ b) for b in bits]
        ranks = add_up(ranks, *others).astype(bf16)
    rank = FACTOR_RANK
    decoder_query, decoder_output = ranks[:, :rank], ranks[:, rank : 2 * rank]
    query_backward, output_backward = ranks[:, 2 * rank : 3 * rank], ranks[:, 3 * rank :]
    gradients = jnp.stack(
        [
            leading_contraction(query_backward, training_input),
            leading_contraction(output_backward, attention_mixed),
            leading_contraction(decoder_query, query_cotangent),
            leading_contraction(decoder_output, output_cotangent),
        ]
    ).astype(bf16)
    width = gradients.shape[-1]
    by_core = gradients.reshape(8, 2, 16, width)
    summed = cores_summed(by_core, core).reshape(4, 2, 16, width)
    own_part = scatter_xy(lambda d: pick(summed, (at_x + d) % 4), half).astype(bf16)
    around = gather_xy(own_part, half)
    both = jnp.stack(in_order(around, other_core(around), core), axis=2)
    twice = jnp.concatenate([both, both], axis=0)
    overall = lax.dynamic_slice_in_dim(twice, (4 - at_x) % 4, 4, 0).reshape(4, rank, width)
    overall = adapter_factor * overall.astype(jnp.float32)
    refreshed_down, refreshed_down_mean, refreshed_down_variance = apply_adam_rule(
        adapter_down, overall[:2], down_mean_moment, down_variance_moment
    )
    refreshed_up, refreshed_up_mean, refreshed_up_variance = apply_adam_rule(
        adapter_up, overall[2:], up_mean_moment, up_variance_moment
    )
    combined_down = refreshed_down.astype(bf16)
    combined_up = refreshed_up.astype(bf16)
    swap = [(i * 16 + j, j * 16 + i) for i in range(16) for j in range(16)]
    down_block = lax.ppermute(combined_down[0], ("dp", "tensor"), swap)
    up_block = lax.ppermute(combined_up[1], ("dp", "tensor"), swap)

    gain = norm_multiplier.astype(jnp.float32)[:, None]
    weight_all = (
        jnp.concatenate([query_weight, key_weight, value_weight], axis=1).astype(jnp.float32) * gain
    ).astype(bf16)
    down_scaled = (down_block.astype(jnp.float32) * gain[:, 0]).astype(bf16)
    count = rows.shape[0]
    sums, squares = [], []
    for block in gathered:
        flat = block.reshape(2 * count, -1)
        part = jnp.dot(flat, weight_all, preferred_element_type=jnp.float32).astype(bf16)
        sums.append(cores_summed(part.reshape(1, 2, count, -1), core_differs)[0])
        wide = flat.astype(jnp.float32)
        squares.append(jnp.sum(wide * wide, axis=1, keepdims=True))
    sums = jnp.stack(sums)

    def for_x(blocks):
        def block(d):
            first = (2 * ((at_x + d) % 4) - at_z) % 8
            return jnp.stack([pick(blocks, slot_of[first]), pick(blocks, slot_of[(first + 1) % 8])])

        return block

    base = scatter_xy(for_x(sums), half)

    everything = jnp.stack(gathered).reshape(16 * count, -1)
    low_rank = contract_last(everything, down_scaled)
    extra = jnp.concatenate(
        [low_rank, jnp.broadcast_to(jnp.concatenate(squares, axis=0), low_rank.shape)], axis=1
    ).reshape(8, 2, count, 2 * rank)
    extra = scatter_xy(for_x(cores_summed(extra, core_differs)), half)
    low_rank = extra[:, :rank].astype(bf16)
    inverse = lax.rsqrt(extra[:, rank : rank + 1] / MODEL_WIDTH + NORM_EPS)
    head_cols = query_weight.shape[1]
    kv_cols = key_weight.shape[1]
    change = adapter_factor * jnp.dot(low_rank, combined_up[0], preferred_element_type=jnp.float32)
    projected = jnp.concatenate([base[:, :head_cols] + change, base[:, head_cols:]], axis=1)
    projected = jnp.where(inverse > 0.0, projected * inverse, 0.0).astype(bf16)
    local_row = key_value_cache.shape[0]
    step_rows = count // STEPS
    mine = jnp.concatenate([projected[:step_rows], projected[step_rows:]], axis=1)
    mine = mine.reshape(16, local_row, -1)
    heads = lax.all_to_all(mine, "tensor", split_axis=0, concat_axis=0)
    heads = heads.reshape(16, local_row, STEPS, head_cols + 2 * kv_cols)
    queries = heads[..., :head_cols].reshape(
        KEY_VALUE_HEADS, 2, local_row, STEPS, head_cols // HEAD_WIDTH, HEAD_WIDTH
    )
    queries = queries.transpose(2, 0, 3, 1, 4, 5).reshape(
        local_row, KEY_VALUE_HEADS, STEPS * QUERY_HEADS // KEY_VALUE_HEADS, HEAD_WIDTH
    )
    fresh = heads[..., head_cols:].reshape(KEY_VALUE_HEADS, 2, local_row, STEPS, 2, kv_cols)
    fresh = fresh.transpose(4, 2, 3, 0, 1, 5).reshape(
        2, local_row, STEPS, KEY_VALUE_HEADS, HEAD_WIDTH
    )
    cache_of_keys = key_value_cache[:, :, 0, :].reshape(
        local_row, CACHE_SLOTS, KEY_VALUE_HEADS, HEAD_WIDTH
    )
    cache_of_values = key_value_cache[:, :, 1, :].reshape(
        local_row, CACHE_SLOTS, KEY_VALUE_HEADS, HEAD_WIDTH
    )
    valid = jnp.arange(CACHE_SLOTS, dtype=jnp.int32)[None, :] < lengths[:, None]
    attended = attend_rows(queries, cache_of_keys, cache_of_values, valid, fresh[0], fresh[1])
    attended = attended.reshape(
        local_row, KEY_VALUE_HEADS, STEPS, 2, head_cols // HEAD_WIDTH, HEAD_WIDTH
    )
    attended = attended.transpose(1, 3, 0, 2, 4, 5).reshape(16, local_row, STEPS * head_cols)
    head_block = lax.all_to_all(attended, "tensor", split_axis=0, concat_axis=0)
    head_block = head_block.reshape(step_rows, STEPS * head_cols)
    head_block = jnp.concatenate([head_block[:, :head_cols], head_block[:, head_cols:]], axis=0)

    output_combined = (
        output_weight.astype(jnp.float32)
        + adapter_factor * leading_contraction(combined_down[1], up_block)
    ).astype(bf16)
    around = gather_xy(head_block, half)
    all_heads = jnp.stack([around, other_core(around)], axis=2)
    out_cols = output_weight.shape[1]
    terms = jnp.dot(
        all_heads.reshape(16 * count, head_cols), output_combined, preferred_element_type=jnp.float32
    )
    terms = terms.astype(bf16).reshape(8, 2, count, out_cols)

    def for_z(d):
        target = (at_z + d) % 8
        return pick(terms, (2 * at_x_of(target) + target % 2) % 8)

    def at_x_of(target):
        return (target // 2 - at_x) % 4

    far = for_z(4)
    low, high = z_up(far[0]), z_down(far[1])
    ahead, behind = for_z(3), for_z(5)
    up = jnp.stack([add_up(ahead[0], low).astype(bf16), ahead[1]])
    down = jnp.stack([behind[0], add_up(behind[1], high).astype(bf16)])
    for d in (2, 1):
        up = add_up(for_z(d), z_up(up)).astype(bf16)
        down = add_up(for_z(8 - d), z_down(down)).astype(bf16)
    total = add_up(for_z(0), z_up(up), z_down(down))
    kept, sent = pick(total, core_differs), pick(total, 1 - core_differs).astype(bf16)
    attn_out = add_up(kept, other_y(sent)).astype(bf16)
    return (
        attn_out.reshape(STEPS, step_rows, out_cols),
        refreshed_down,
        refreshed_up,
        refreshed_down_mean,
        refreshed_up_mean,
        refreshed_down_variance,
        refreshed_up_variance,
    )


def solution(mesh):
    in_specs = (
        P(None, "tensor", "dp"),
        P("dp"),
        P("dp", "tensor"),
        P("dp", "tensor"),
        P("dp", "tensor"),
        P("tensor", "dp"),
        P(("dp", "tensor"), None, None, None),
        P(("dp", "tensor")),
        P("dp", "tensor"),
        P("dp", "tensor"),
        P("dp", "tensor"),
        P("dp", "tensor"),
        P(),
        P(None, None, "tensor"),
        P(None, None, "tensor"),
        P(None, None, "tensor"),
        P(None, None, "tensor"),
        P(None, None, "tensor"),
        P(None, None, "tensor"),
    )
    out_specs = (
        P(None, "tensor", "dp"),
        P(None, None, "tensor"),
        P(None, None, "tensor"),
        P(None, None, "tensor"),
        P(None, None, "tensor"),
        P(None, None, "tensor"),
        P(None, None, "tensor"),
    )
    return jax.shard_map(
        on_device, mesh=mesh, in_specs=in_specs, out_specs=out_specs, check_vma=False
    )
```

```python
import math

import jax
import jax.numpy as jnp
from jax import lax
from jax.experimental import pallas as pl
from jax.experimental.pallas import tpu as pltpu
from jax.sharding import PartitionSpec as P

MODEL_WIDTH = 16384
QUERY_HEADS = 128
HEAD_WIDTH = 128
KEY_VALUE_HEADS = 8
FACTOR_RANK = 64
STEPS = 2
CACHE_SLOTS = 128
SEQLEN = 64
GROUP = 8


BETA_ONE = 0.9
BETA_TWO = 0.999
BIAS_ONE = 0.271
BIAS_TWO = 0.002997001
LEARN_RATE = 0.3
ADAM_EPS = 1e-08
NORM_EPS = 1e-05
NEG_FILL = -1e30


def apply_adam_rule(parameter, gradient, first_moment, second_moment):
    moment_one = BETA_ONE * first_moment.astype(jnp.float32) + (1.0 - BETA_ONE) * gradient
    moment_two = (
        BETA_TWO * second_moment.astype(jnp.float32) + (1.0 - BETA_TWO) * gradient * gradient
    )
    change = moment_one / BIAS_ONE / (jnp.sqrt(moment_two / BIAS_TWO) + ADAM_EPS)
    return (
        parameter - LEARN_RATE * change,
        moment_one.astype(jnp.bfloat16),
        moment_two.astype(jnp.bfloat16),
    )


def leading_contraction(lhs_array, rhs_array):
    return lax.dot_general(
        lhs_array, rhs_array, (((0,), (0,)), ((), ())), preferred_element_type=jnp.float32
    )


def contract_last(lhs_array, rhs_array):
    return lax.dot_general(
        lhs_array, rhs_array, (((1,), (1,)), ((), ())), preferred_element_type=jnp.float32
    )


def attend_rows(query_rows, cache_of_keys, cache_of_values, valid, latest_keys, latest_values):
    scale_att = 1.0 / math.sqrt(HEAD_WIDTH)
    cache_scores = (
        jnp.einsum("rkgd,rpkd->rkgp", query_rows, cache_of_keys, preferred_element_type=jnp.float32)
        * scale_att
    )
    cache_scores = jnp.where(valid[:, None, None, :], cache_scores, NEG_FILL)
    fresh_scores = (
        jnp.einsum("rkgd,rpkd->rkgp", query_rows, latest_keys, preferred_element_type=jnp.float32)
        * scale_att
    )
    group = QUERY_HEADS // KEY_VALUE_HEADS
    query_step = jnp.arange(STEPS * group, dtype=jnp.int32) // group
    seen = jnp.arange(STEPS, dtype=jnp.int32)[None, :] <= query_step[:, None]
    fresh_scores = jnp.where(seen[None, None], fresh_scores, NEG_FILL)
    scores = jnp.concatenate([cache_scores, fresh_scores], axis=-1)
    row_top = jnp.max(scores, axis=-1, keepdims=True)
    exponent = jnp.exp(scores - row_top)
    attention_weights = (exponent / jnp.sum(exponent, axis=-1, keepdims=True)).astype(jnp.bfloat16)
    cache_part = jnp.einsum(
        "rkgp,rpkd->rkgd",
        attention_weights[..., :CACHE_SLOTS],
        cache_of_values,
        preferred_element_type=jnp.float32,
    )
    fresh_part = jnp.einsum(
        "rkgp,rpkd->rkgd",
        attention_weights[..., CACHE_SLOTS:],
        latest_values,
        preferred_element_type=jnp.float32,
    )
    return (cache_part + fresh_part).astype(jnp.bfloat16)


VMEM = pl.BlockSpec(memory_space=pltpu.VMEM)
SMEM = pl.BlockSpec(memory_space=pltpu.SMEM)
ANY = pl.BlockSpec(memory_space=pl.ANY)


def call(kernel, out_shape, inputs, in_specs=None, flops=0, scratch=(), vmem=24):
    moved = sum(a.size * a.dtype.itemsize for a in (*inputs, *out_shape))
    return pl.pallas_call(
        kernel,
        out_shape=out_shape,
        in_specs=in_specs or [VMEM] * len(inputs),
        out_specs=[VMEM] * len(out_shape),
        scratch_shapes=list(scratch),
        compiler_params=pltpu.CompilerParams(vmem_limit_bytes=vmem * 2**20),
        cost_estimate=pl.CostEstimate(flops=flops, bytes_accessed=moved, transcendentals=0),
    )(*inputs)


def shape(dims, kind):
    return jax.ShapeDtypeStruct(dims, kind)


def rank_kernel(rewards, *refs):
    sources, (ranks, query_cot, out_cot), copies = refs[:6], refs[6:9], refs[9:15]
    started = [
        pltpu.make_async_copy(source, copy, refs[15].at[number])
        for number, (source, copy) in enumerate(zip(sources, copies))
    ]
    for copy in started:
        copy.start()
    for copy in started:
        copy.wait()
    inputs, query_grad, mixed, out_grad, down, up = copies
    tokens = inputs.shape[0]
    first = lax.axis_index("dp") * (tokens // SEQLEN)
    group = (first // GROUP) * GROUP
    total = rewards[group]
    for member in range(1, GROUP):
        total = total + rewards[group + member]
    mean = total.astype(jnp.float32) * (1.0 / GROUP)
    for seq in range(tokens // SEQLEN):
        weight = rewards[first + seq].astype(jnp.float32) - mean
        span = slice(seq * SEQLEN, (seq + 1) * SEQLEN)
        query_cot[span, :] = (weight * query_grad[span, :].astype(jnp.float32)).astype(jnp.bfloat16)
        out_cot[span, :] = (weight * out_grad[span, :].astype(jnp.float32)).astype(jnp.bfloat16)
    ranks[...] = jnp.concatenate(
        [
            contract_last(inputs[...], down[0].astype(jnp.bfloat16)),
            contract_last(mixed[...], down[1].astype(jnp.bfloat16)),
            contract_last(query_cot[...], up[0].astype(jnp.bfloat16)),
            contract_last(out_cot[...], up[1].astype(jnp.bfloat16)),
        ],
        axis=1,
    ).astype(jnp.bfloat16)


def gradient_kernel(own, one, two, three, inputs, mixed, query_cot, out_cot, *refs):
    keep, send = refs[-2:]
    ranks = add_up(own[...], one[...], two[...], three[...])
    turned = ranks.T.astype(jnp.bfloat16)
    rank = FACTOR_RANK
    core = lax.axis_index("dp") % 2
    order = ((2, inputs), (3, mixed), (0, query_cot), (1, out_cot))
    for place, (which, other) in enumerate(order):
        part = jnp.dot(
            turned[which * rank : (which + 1) * rank],
            other[...],
            preferred_element_type=jnp.float32,
        ).astype(jnp.bfloat16)
        for block in range(rank // 32):
            even = part[block * 32 : block * 32 + 16]
            odd = part[block * 32 + 16 : block * 32 + 32]
            at = place * (rank // 32) + block
            keep[at] = jnp.where(core == 0, even, odd)
            send[at] = jnp.where(core == 0, odd, even)


def project_kernel(count, *refs):
    blocks, (query, key_turned, value_turned) = refs[:count], refs[count : count + 3]
    keep, send = refs[-2:]
    rows = blocks[0].shape[1]
    head_cols, kv_cols = query.shape[1], key_turned.shape[0]
    lhs = jnp.concatenate([b[side] for side in (0, 1) for b in blocks], axis=0)
    tile = 256

    def store(result, start, stop):
        result = result.astype(jnp.bfloat16)
        for at in range(count):
            keep[at, :, start:stop] = result[at * rows : (at + 1) * rows]
            other = (count + at) * rows
            send[at, :, start:stop] = result[other : other + rows]

    for start in range(0, head_cols, tile):
        part = jnp.dot(lhs, query[:, start : start + tile], preferred_element_type=jnp.float32)
        store(part, start, start + tile)
    turned = jnp.concatenate([key_turned[...], value_turned[...]], axis=0)
    store(contract_last(lhs, turned), head_cols, head_cols + 2 * kv_cols)


def spread_kernel(kept, received, *refs):
    at_x = lax.axis_index("dp") // 4
    for distance, out in enumerate(refs[-4:]):
        x = lax.rem(at_x + distance, 4)
        for half in range(2):
            out[half] = add_up(kept[2 * x + half], received[2 * x + half]).astype(out.dtype)


def sum_kernel(count, *refs):
    refs[-1][...] = add_up(*[ref[...] for ref in refs[:count]]).astype(refs[-1].dtype)


def join_kernel(kept, received, own, one, two, three, up_zero, _, out):
    rank = up_zero.shape[0]
    extra = add_up(own[...], one[...], two[...], three[...])
    inverse = lax.rsqrt(extra[:, rank : rank + 1] / MODEL_WIDTH + NORM_EPS)
    low_rank = extra[:, :rank].astype(jnp.bfloat16)
    adapter_factor = 1.0 / math.sqrt(MODEL_WIDTH * FACTOR_RANK)
    head_cols, cols = up_zero.shape[1], kept.shape[1]
    step_rows = out.shape[0]
    change = adapter_factor * jnp.dot(
        low_rank, up_zero[...], preferred_element_type=jnp.float32
    )
    base = add_up(kept[...], received[...])
    for start, stop, value in (
        (0, head_cols, base[:, :head_cols] + change),
        (head_cols, cols, base[:, head_cols:]),
    ):
        value = jnp.where(inverse > 0.0, value * inverse, 0.0).astype(jnp.bfloat16)
        for step in range(STEPS):
            out[:, step * cols + start : step * cols + stop] = value[
                step * step_rows : (step + 1) * step_rows
            ]


def adam_kernel(own, other, rows, *refs):
    (down, up, down_mean, up_mean, down_var, up_var), outs = refs[:6], refs[-11:]
    new_down, new_up, new_down_mean, new_up_mean, new_down_var, new_up_var = outs[:6]
    down_zero, down_one, up_zero, up_one, products = outs[6:]
    dp = lax.axis_index("dp")
    at_x, core = dp // 4, dp % 2
    adapter_factor = 1.0 / math.sqrt(MODEL_WIDTH * FACTOR_RANK)
    old = ((down, down_mean, down_var), (up, up_mean, up_var))
    new = ((new_down, new_down_mean, new_down_var), (new_up, new_up_mean, new_up_var))
    low = ((down_zero, down_one), (up_zero, up_one))
    for factor in range(4):
        side, which = factor // 2, factor % 2
        distance = lax.rem(factor - at_x + 4, 4)
        for half in range(2):
            mine, theirs = own[distance, half], other[distance, half]
            pair = (jnp.where(core == 0, mine, theirs), jnp.where(core == 0, theirs, mine))
            for number in range(2):
                at = (half * 2 + number) * 16
                span = slice(at, at + 16)
                gradient = adapter_factor * pair[number].astype(jnp.float32)
                result = apply_adam_rule(
                    old[side][0][which, span],
                    gradient,
                    old[side][1][which, span],
                    old[side][2][which, span],
                )
                for target, value in zip(new[side], result):
                    target[which, span] = value
                low[side][which][span] = result[0].astype(jnp.bfloat16)
    count = products.shape[0]
    rank = down_zero.shape[0]
    raw = rows[:count].astype(jnp.float32)
    scaled = (raw * rows[count : count + 1].astype(jnp.float32)).astype(jnp.bfloat16)
    factor = down_zero[...]
    product = contract_last(scaled, jnp.concatenate([factor, jnp.zeros_like(factor)], axis=0))
    squares = jnp.sum(raw * raw, axis=1, keepdims=True)
    lane = lax.broadcasted_iota(jnp.int32, product.shape, 1)
    products[...] = jnp.where(lane < rank, product, squares)


def output_kernel(own, other, weight, terms):
    rows, depth = own.shape[2], own.shape[3]
    lhs = jnp.concatenate(
        [ref[x, half] for x in range(4) for half in range(2) for ref in (own, other)], axis=0
    )
    tile = 256
    for start in range(0, weight.shape[1], tile):
        part = jnp.dot(lhs, weight[:, start : start + tile], preferred_element_type=jnp.float32)
        part = part.astype(jnp.bfloat16)
        for at in range(16):
            terms[at // 2, at % 2, :, start : start + tile] = part[at * rows : (at + 1) * rows]


def hop_dp(array, target):
    return lax.ppermute(array, "dp", [(s, target(s)) for s in range(16)])


def hop_tensor(array, target):
    return lax.ppermute(array, "tensor", [(s, target(s)) for s in range(16)])


def other_core(array):
    return hop_dp(array, lambda s: s ^ 1)


def other_half(array):
    return hop_dp(array, lambda s: s ^ 2)


def x_up(array):
    return hop_dp(array, lambda s: (s + 4) % 16)


def x_down(array):
    return hop_dp(array, lambda s: (s - 4) % 16)


def x_far(array):
    return hop_dp(array, lambda s: (s + 8) % 16)


def other_y(array):
    return hop_tensor(array, lambda s: s ^ 1)


def z_up(array):
    return hop_tensor(array, lambda s: (s + 2) % 16)


def z_down(array):
    return hop_tensor(array, lambda s: (s - 2) % 16)


def pick(array, index, axis=0):
    return lax.dynamic_index_in_dim(array, index, axis, keepdims=False)


def add_up(*arrays):
    total = arrays[0].astype(jnp.float32)
    for array in arrays[1:]:
        total = total + array.astype(jnp.float32)
    return total


def cores_summed(kept, sent):
    return add_up(kept, other_core(sent)).astype(kept.dtype)


def scatter_xy(block, half):
    kind = block(0).dtype
    far, ahead, behind = block(2), block(1), block(3)
    low, high = x_up(far[0]), x_down(far[1])
    ahead = jnp.stack([add_up(ahead[0], low).astype(kind), ahead[1]])
    behind = jnp.stack([behind[0], add_up(behind[1], high).astype(kind)])
    total = add_up(block(0), x_up(ahead), x_down(behind))
    kept, sent = pick(total, half), pick(total, 1 - half).astype(kind)
    return kept, other_half(sent)


def in_order(own, other, position):
    first = jnp.where(position == 0, own, other)
    second = jnp.where(position == 0, other, own)
    return first, second


def gather_xy(array, half):
    own = jnp.stack(in_order(array, other_half(array), half))
    behind, ahead = x_up(own), x_down(own)
    far = jnp.stack([x_up(behind[0]), x_down(ahead[1])])
    return jnp.stack([own, ahead, far, behind])


def on_device(
    decoder_input,
    norm_multiplier,
    query_weight,
    key_weight,
    value_weight,
    output_weight,
    key_value_cache,
    lengths,
    training_input,
    query_gradient,
    attention_mixed,
    output_gradient,
    rewards,
    adapter_down,
    adapter_up,
    down_mean_moment,
    up_mean_moment,
    down_variance_moment,
    up_variance_moment,
):
    adapter_factor = 1.0 / math.sqrt(MODEL_WIDTH * FACTOR_RANK)
    dp_index = lax.axis_index("dp")
    tensor_index = lax.axis_index("tensor")
    at_x, half, core = dp_index // 4, (dp_index // 2) % 2, dp_index % 2
    at_z, at_y = tensor_index // 2, tensor_index % 2
    core_differs = core ^ at_y
    bf16 = jnp.bfloat16

    gain = norm_multiplier.astype(jnp.float32)[None, :]
    raw = decoder_input.reshape(STEPS * decoder_input.shape[1], -1)
    rows = (raw.astype(jnp.float32) * gain).astype(bf16)
    count = rows.shape[0]
    swap = [(i * 16 + j, j * 16 + i) for i in range(16) for j in range(16)]
    raw = jnp.concatenate([raw, jnp.broadcast_to(norm_multiplier[None, :], (16, raw.shape[1]))])
    turned_rows = lax.ppermute(raw, ("dp", "tensor"), swap)
    own = jnp.stack(in_order(rows, other_y(rows), core_differs))
    gathered = [own]
    up, down = own, own
    for _ in range(3):
        up, down = z_up(up), z_down(down)
        gathered += [up, down]
    gathered.append(jnp.stack([z_up(up[0]), z_down(down[1])]))

    def slot_of(distance):
        return jnp.where(distance < 4, 2 * distance, 15 - 2 * distance)

    tokens, width = training_input.shape
    rank = FACTOR_RANK
    ranks, query_cotangent, output_cotangent = call(
        rank_kernel,
        (shape((tokens, 4 * rank), bf16), shape((tokens, width), bf16), shape((tokens, width), bf16)),
        (
            rewards,
            training_input,
            query_gradient,
            attention_mixed,
            output_gradient,
            adapter_down,
            adapter_up,
        ),
        in_specs=[SMEM] + [ANY] * 6,
        flops=8 * tokens * width * rank,
        scratch=[pltpu.VMEM((tokens, width), bf16)] * 4
        + [pltpu.VMEM((2, rank, width), jnp.float32)] * 2
        + [pltpu.SemaphoreType.DMA((6,))],
        vmem=56,
    )
    others = [hop_tensor(ranks, lambda s, b=b: s ^ b) for b in (1, 2, 3)]
    ranks = add_up(ranks, *others).astype(bf16)
    others = [hop_tensor(ranks, lambda s, b=b: s ^ b) for b in (4, 8, 12)]
    kept, sent = call(
        gradient_kernel,
        (shape((8, 16, width), bf16), shape((8, 16, width), bf16)),
        (
            ranks,
            *others,
            training_input,
            attention_mixed,
            query_cotangent,
            output_cotangent,
            *gathered[1:3],
        ),
        in_specs=[VMEM] * 8 + [ANY] * 2,
        flops=8 * tokens * width * rank,
    )
    block = (2, 16, width)
    near, ahead, far, behind = call(
        spread_kernel,
        (shape(block, jnp.float32), *[shape(block, bf16)] * 3),
        (kept, other_core(sent), *gathered[3:5]),
        in_specs=[VMEM] * 2 + [ANY] * 2,
    )
    (total,) = call(
        lambda *refs: sum_kernel(4, *refs),
        (shape(block, bf16),),
        (near, x_up(ahead), x_far(far), x_down(behind), *gathered[5:7]),
        in_specs=[VMEM] * 4 + [ANY] * 2,
    )
    (total,) = call(
        lambda *refs: sum_kernel(2, *refs),
        (shape(block, bf16),),
        (total, other_half(total), gathered[7]),
        in_specs=[VMEM] * 2 + [ANY],
    )
    around = jnp.stack([total, x_down(total), x_far(total), x_up(total)])

    head_cols = query_weight.shape[1]
    kv_cols = key_weight.shape[1]
    sums = []
    for first, last in ((0, 3), (3, 5), (5, 8)):
        number = last - first
        cols = head_cols + 2 * kv_cols
        kept, sent = call(
            lambda *refs, number=number: project_kernel(number, *refs),
            (shape((number, count, cols), bf16), shape((number, count, cols), bf16)),
            (*gathered[first:last], query_weight, key_weight.T, value_weight.T),
            flops=4 * number * count * width * cols,
        )
        sums.append(cores_summed(kept, sent))
    adam = call(
        adam_kernel,
        (
            *[shape(adapter_down.shape, jnp.float32)] * 2,
            *[shape(adapter_down.shape, bf16)] * 4,
            *[shape((rank, width), bf16)] * 4,
            shape((count, 2 * rank), jnp.float32),
        ),
        (
            around,
            other_core(around),
            turned_rows,
            adapter_down,
            adapter_up,
            down_mean_moment,
            up_mean_moment,
            down_variance_moment,
            up_variance_moment,
            kept,
        ),
        in_specs=[VMEM] * 9 + [ANY],
        flops=2 * count * width * 2 * rank,
    )
    refreshed_down, refreshed_up = adam[:2]
    refreshed_down_mean, refreshed_up_mean = adam[2:4]
    refreshed_down_variance, refreshed_up_variance = adam[4:6]
    down_one, up_zero, up_one, extra = adam[7:]
    up_block = lax.ppermute(up_one, ("dp", "tensor"), swap)
    others = [hop_tensor(extra, lambda s, b=b: s ^ b) for b in (1, 2, 3)]
    extra = add_up(extra, *others)
    others = [hop_tensor(extra, lambda s, b=b: s ^ b) for b in (4, 8, 12)]
    sums = jnp.concatenate(sums)

    def for_x(blocks):
        def block(d):
            first = (2 * ((at_x + d) % 4) - at_z) % 8
            return jnp.stack([pick(blocks, slot_of(first)), pick(blocks, slot_of((first + 1) % 8))])

        return block

    kept, received = scatter_xy(for_x(sums), half)
    local_row = key_value_cache.shape[0]
    step_rows = count // STEPS
    (mine,) = call(
        join_kernel,
        (shape((step_rows, STEPS * (head_cols + 2 * kv_cols)), bf16),),
        (kept, received, extra, *others, up_zero, up_block),
        in_specs=[VMEM] * 7 + [ANY],
    )
    mine = mine.reshape(16, local_row, -1)
    heads = lax.all_to_all(mine, "tensor", split_axis=0, concat_axis=0)
    heads = heads.reshape(16, local_row, STEPS, head_cols + 2 * kv_cols)
    queries = heads[..., :head_cols].reshape(
        KEY_VALUE_HEADS, 2, local_row, STEPS, head_cols // HEAD_WIDTH, HEAD_WIDTH
    )
    queries = queries.transpose(2, 0, 3, 1, 4, 5).reshape(
        local_row, KEY_VALUE_HEADS, STEPS * QUERY_HEADS // KEY_VALUE_HEADS, HEAD_WIDTH
    )
    fresh = heads[..., head_cols:].reshape(KEY_VALUE_HEADS, 2, local_row, STEPS, 2, kv_cols)
    fresh = fresh.transpose(4, 2, 3, 0, 1, 5).reshape(
        2, local_row, STEPS, KEY_VALUE_HEADS, HEAD_WIDTH
    )
    cache_of_keys = key_value_cache[:, :, 0, :].reshape(
        local_row, CACHE_SLOTS, KEY_VALUE_HEADS, HEAD_WIDTH
    )
    cache_of_values = key_value_cache[:, :, 1, :].reshape(
        local_row, CACHE_SLOTS, KEY_VALUE_HEADS, HEAD_WIDTH
    )
    valid = jnp.arange(CACHE_SLOTS, dtype=jnp.int32)[None, :] < lengths[:, None]
    attended = attend_rows(queries, cache_of_keys, cache_of_values, valid, fresh[0], fresh[1])
    attended = attended.reshape(
        local_row, KEY_VALUE_HEADS, STEPS, 2, head_cols // HEAD_WIDTH, HEAD_WIDTH
    )
    attended = attended.transpose(1, 3, 0, 2, 4, 5).reshape(16, local_row, STEPS * head_cols)
    head_block = lax.all_to_all(attended, "tensor", split_axis=0, concat_axis=0)
    head_block = head_block.reshape(step_rows, STEPS * head_cols)
    output_combined = (
        output_weight.astype(jnp.float32)
        + adapter_factor * leading_contraction(down_one, up_block)
    ).astype(bf16)
    out_cols = output_weight.shape[1]
    results = []
    for step in range(STEPS):
        own = head_block[:, step * head_cols : (step + 1) * head_cols]
        around = gather_xy(own, half)
        (terms,) = call(
            output_kernel,
            (shape((8, 2, step_rows, out_cols), bf16),),
            (around, other_core(around), output_combined),
            flops=32 * step_rows * head_cols * out_cols,
        )

        def for_z(d, terms=terms):
            target = (at_z + d) % 8
            return pick(terms, 2 * ((target // 2 - at_x) % 4) + target % 2)

        far = for_z(4)
        low, high = z_up(far[0]), z_down(far[1])
        ahead, behind = for_z(3), for_z(5)
        up = jnp.stack([add_up(ahead[0], low).astype(bf16), ahead[1]])
        down = jnp.stack([behind[0], add_up(behind[1], high).astype(bf16)])
        for d in (2, 1):
            up = add_up(for_z(d), z_up(up)).astype(bf16)
            down = add_up(for_z(8 - d), z_down(down)).astype(bf16)
        total = add_up(for_z(0), z_up(up), z_down(down))
        kept, sent = pick(total, core_differs), pick(total, 1 - core_differs).astype(bf16)
        results.append(add_up(kept, other_y(sent)).astype(bf16))
    return (
        jnp.stack(results),
        refreshed_down,
        refreshed_up,
        refreshed_down_mean,
        refreshed_up_mean,
        refreshed_down_variance,
        refreshed_up_variance,
    )


def solution(mesh):
    in_specs = (
        P(None, "tensor", "dp"),
        P("dp"),
        P("dp", "tensor"),
        P("dp", "tensor"),
        P("dp", "tensor"),
        P("tensor", "dp"),
        P(("dp", "tensor"), None, None, None),
        P(("dp", "tensor")),
        P("dp", "tensor"),
        P("dp", "tensor"),
        P("dp", "tensor"),
        P("dp", "tensor"),
        P(),
        P(None, None, "tensor"),
        P(None, None, "tensor"),
        P(None, None, "tensor"),
        P(None, None, "tensor"),
        P(None, None, "tensor"),
        P(None, None, "tensor"),
    )
    out_specs = (
        P(None, "tensor", "dp"),
        P(None, None, "tensor"),
        P(None, None, "tensor"),
        P(None, None, "tensor"),
        P(None, None, "tensor"),
        P(None, None, "tensor"),
        P(None, None, "tensor"),
    )
    return jax.shard_map(
        on_device, mesh=mesh, in_specs=in_specs, out_specs=out_specs, check_vma=False
    )
```

```python
import math

import jax
import jax.numpy as jnp
from jax import lax
from jax.experimental import pallas as pl
from jax.experimental.pallas import tpu as pltpu
from jax.sharding import PartitionSpec as P

MODEL_WIDTH = 16384
QUERY_HEADS = 128
HEAD_WIDTH = 128
KEY_VALUE_HEADS = 8
FACTOR_RANK = 64
STEPS = 2
CACHE_SLOTS = 128
SEQLEN = 64
GROUP = 8


BETA_ONE = 0.9
BETA_TWO = 0.999
BIAS_ONE = 0.271
BIAS_TWO = 0.002997001
LEARN_RATE = 0.3
ADAM_EPS = 1e-08
NORM_EPS = 1e-05
NEG_FILL = -1e30


def apply_adam_rule(parameter, gradient, first_moment, second_moment):
    moment_one = BETA_ONE * first_moment.astype(jnp.float32) + (1.0 - BETA_ONE) * gradient
    moment_two = (
        BETA_TWO * second_moment.astype(jnp.float32) + (1.0 - BETA_TWO) * gradient * gradient
    )
    change = moment_one / BIAS_ONE / (jnp.sqrt(moment_two / BIAS_TWO) + ADAM_EPS)
    return (
        parameter - LEARN_RATE * change,
        moment_one.astype(jnp.bfloat16),
        moment_two.astype(jnp.bfloat16),
    )


def leading_contraction(lhs_array, rhs_array):
    return lax.dot_general(
        lhs_array, rhs_array, (((0,), (0,)), ((), ())), preferred_element_type=jnp.float32
    )


def contract_last(lhs_array, rhs_array):
    return lax.dot_general(
        lhs_array, rhs_array, (((1,), (1,)), ((), ())), preferred_element_type=jnp.float32
    )


def attend_rows(query_rows, cache_of_keys, cache_of_values, valid, latest_keys, latest_values):
    scale_att = 1.0 / math.sqrt(HEAD_WIDTH)
    cache_scores = (
        jnp.einsum("rkgd,rpkd->rkgp", query_rows, cache_of_keys, preferred_element_type=jnp.float32)
        * scale_att
    )
    cache_scores = jnp.where(valid[:, None, None, :], cache_scores, NEG_FILL)
    fresh_scores = (
        jnp.einsum("rkgd,rpkd->rkgp", query_rows, latest_keys, preferred_element_type=jnp.float32)
        * scale_att
    )
    group = QUERY_HEADS // KEY_VALUE_HEADS
    query_step = jnp.arange(STEPS * group, dtype=jnp.int32) // group
    seen = jnp.arange(STEPS, dtype=jnp.int32)[None, :] <= query_step[:, None]
    fresh_scores = jnp.where(seen[None, None], fresh_scores, NEG_FILL)
    scores = jnp.concatenate([cache_scores, fresh_scores], axis=-1)
    row_top = jnp.max(scores, axis=-1, keepdims=True)
    exponent = jnp.exp(scores - row_top)
    attention_weights = (exponent / jnp.sum(exponent, axis=-1, keepdims=True)).astype(jnp.bfloat16)
    cache_part = jnp.einsum(
        "rkgp,rpkd->rkgd",
        attention_weights[..., :CACHE_SLOTS],
        cache_of_values,
        preferred_element_type=jnp.float32,
    )
    fresh_part = jnp.einsum(
        "rkgp,rpkd->rkgd",
        attention_weights[..., CACHE_SLOTS:],
        latest_values,
        preferred_element_type=jnp.float32,
    )
    return (cache_part + fresh_part).astype(jnp.bfloat16)


VMEM = pl.BlockSpec(memory_space=pltpu.VMEM)
SMEM = pl.BlockSpec(memory_space=pltpu.SMEM)
ANY = pl.BlockSpec(memory_space=pl.ANY)


def call(kernel, out_shape, inputs, in_specs=None, flops=0, scratch=(), vmem=24):
    moved = sum(a.size * a.dtype.itemsize for a in (*inputs, *out_shape))
    return pl.pallas_call(
        kernel,
        out_shape=out_shape,
        in_specs=in_specs or [VMEM] * len(inputs),
        out_specs=[VMEM] * len(out_shape),
        scratch_shapes=list(scratch),
        compiler_params=pltpu.CompilerParams(vmem_limit_bytes=vmem * 2**20),
        cost_estimate=pl.CostEstimate(flops=flops, bytes_accessed=moved, transcendentals=0),
    )(*inputs)


def shape(dims, kind):
    return jax.ShapeDtypeStruct(dims, kind)


def rank_kernel(rewards, *refs):
    sources, (ranks, query_cot, out_cot), copies = refs[:6], refs[6:9], refs[9:15]
    started = [
        pltpu.make_async_copy(source, copy, refs[15].at[number])
        for number, (source, copy) in enumerate(zip(sources, copies))
    ]
    for copy in started:
        copy.start()
    for copy in started:
        copy.wait()
    inputs, query_grad, mixed, out_grad, down, up = copies
    tokens = inputs.shape[0]
    first = lax.axis_index("dp") * (tokens // SEQLEN)
    group = (first // GROUP) * GROUP
    total = rewards[group]
    for member in range(1, GROUP):
        total = total + rewards[group + member]
    mean = total.astype(jnp.float32) * (1.0 / GROUP)
    for seq in range(tokens // SEQLEN):
        weight = rewards[first + seq].astype(jnp.float32) - mean
        span = slice(seq * SEQLEN, (seq + 1) * SEQLEN)
        query_cot[span, :] = (weight * query_grad[span, :].astype(jnp.float32)).astype(jnp.bfloat16)
        out_cot[span, :] = (weight * out_grad[span, :].astype(jnp.float32)).astype(jnp.bfloat16)
    ranks[...] = jnp.concatenate(
        [
            contract_last(inputs[...], down[0].astype(jnp.bfloat16)),
            contract_last(mixed[...], down[1].astype(jnp.bfloat16)),
            contract_last(query_cot[...], up[0].astype(jnp.bfloat16)),
            contract_last(out_cot[...], up[1].astype(jnp.bfloat16)),
        ],
        axis=1,
    ).astype(jnp.bfloat16)


def gradient_kernel(own, one, two, three, inputs, mixed, query_cot, out_cot, *refs):
    keep, send = refs[-2:]
    ranks = add_up(own[...], one[...], two[...], three[...])
    turned = ranks.T.astype(jnp.bfloat16)
    rank = FACTOR_RANK
    core = lax.axis_index("dp") % 2
    order = ((2, inputs), (3, mixed), (0, query_cot), (1, out_cot))
    for place, (which, other) in enumerate(order):
        part = jnp.dot(
            turned[which * rank : (which + 1) * rank],
            other[...],
            preferred_element_type=jnp.float32,
        ).astype(jnp.bfloat16)
        for block in range(rank // 32):
            even = part[block * 32 : block * 32 + 16]
            odd = part[block * 32 + 16 : block * 32 + 32]
            at = place * (rank // 32) + block
            keep[at] = jnp.where(core == 0, even, odd)
            send[at] = jnp.where(core == 0, odd, even)


def project_kernel(count, *refs):
    blocks, (query, key_turned, value_turned) = refs[:count], refs[count : count + 3]
    keep, send = refs[-2:]
    rows = blocks[0].shape[1]
    head_cols, kv_cols = query.shape[1], key_turned.shape[0]
    lhs = jnp.concatenate([b[side] for side in (0, 1) for b in blocks], axis=0)
    tile = 256

    def store(result, start, stop):
        result = result.astype(jnp.bfloat16)
        for at in range(count):
            keep[at, :, start:stop] = result[at * rows : (at + 1) * rows]
            other = (count + at) * rows
            send[at, :, start:stop] = result[other : other + rows]

    for start in range(0, head_cols, tile):
        part = jnp.dot(lhs, query[:, start : start + tile], preferred_element_type=jnp.float32)
        store(part, start, start + tile)
    turned = jnp.concatenate([key_turned[...], value_turned[...]], axis=0)
    store(contract_last(lhs, turned), head_cols, head_cols + 2 * kv_cols)


def spread_kernel(kept, received, *refs):
    at_x = lax.axis_index("dp") // 4
    for distance, out in enumerate(refs[-4:]):
        x = lax.rem(at_x + distance, 4)
        for half in range(2):
            out[half] = add_up(kept[2 * x + half], received[2 * x + half]).astype(out.dtype)


def sum_kernel(count, *refs):
    refs[-1][...] = add_up(*[ref[...] for ref in refs[:count]]).astype(refs[-1].dtype)


def join_kernel(kept, received, own, one, two, three, up_zero, _, out):
    rank = up_zero.shape[0]
    extra = add_up(own[...], one[...], two[...], three[...])
    inverse = lax.rsqrt(extra[:, rank : rank + 1] / MODEL_WIDTH + NORM_EPS)
    low_rank = extra[:, :rank].astype(jnp.bfloat16)
    adapter_factor = 1.0 / math.sqrt(MODEL_WIDTH * FACTOR_RANK)
    head_cols, cols = up_zero.shape[1], kept.shape[1]
    step_rows = out.shape[0]
    change = adapter_factor * jnp.dot(
        low_rank, up_zero[...], preferred_element_type=jnp.float32
    )
    base = add_up(kept[...], received[...])
    for start, stop, value in (
        (0, head_cols, base[:, :head_cols] + change),
        (head_cols, cols, base[:, head_cols:]),
    ):
        value = jnp.where(inverse > 0.0, value * inverse, 0.0).astype(jnp.bfloat16)
        for step in range(STEPS):
            out[:, step * cols + start : step * cols + stop] = value[
                step * step_rows : (step + 1) * step_rows
            ]


def adam_kernel(own, other, rows, *refs):
    (down, up, down_mean, up_mean, down_var, up_var), outs = refs[:6], refs[-11:]
    new_down, new_up, new_down_mean, new_up_mean, new_down_var, new_up_var = outs[:6]
    down_zero, down_one, up_zero, up_one, products = outs[6:]
    dp = lax.axis_index("dp")
    at_x, core = dp // 4, dp % 2
    adapter_factor = 1.0 / math.sqrt(MODEL_WIDTH * FACTOR_RANK)
    old = ((down, down_mean, down_var), (up, up_mean, up_var))
    new = ((new_down, new_down_mean, new_down_var), (new_up, new_up_mean, new_up_var))
    low = ((down_zero, down_one), (up_zero, up_one))
    for factor in range(4):
        side, which = factor // 2, factor % 2
        distance = lax.rem(factor - at_x + 4, 4)
        for half in range(2):
            mine, theirs = own[distance, half], other[distance, half]
            pair = (jnp.where(core == 0, mine, theirs), jnp.where(core == 0, theirs, mine))
            for number in range(2):
                at = (half * 2 + number) * 16
                span = slice(at, at + 16)
                gradient = adapter_factor * pair[number].astype(jnp.float32)
                result = apply_adam_rule(
                    old[side][0][which, span],
                    gradient,
                    old[side][1][which, span],
                    old[side][2][which, span],
                )
                for target, value in zip(new[side], result):
                    target[which, span] = value
                low[side][which][span] = result[0].astype(jnp.bfloat16)
    count = products.shape[0]
    rank = down_zero.shape[0]
    raw = rows[:count].astype(jnp.float32)
    scaled = (raw * rows[count : count + 1].astype(jnp.float32)).astype(jnp.bfloat16)
    factor = down_zero[...]
    product = contract_last(scaled, jnp.concatenate([factor, jnp.zeros_like(factor)], axis=0))
    squares = jnp.sum(raw * raw, axis=1, keepdims=True)
    lane = lax.broadcasted_iota(jnp.int32, product.shape, 1)
    products[...] = jnp.where(lane < rank, product, squares)


def output_kernel(own, other, weight, terms):
    rows, depth = own.shape[1], weight.shape[0]
    at_z, at_y = lax.axis_index("tensor") // 2, lax.axis_index("tensor") % 2
    core = lax.axis_index("dp") % 2
    lhs = jnp.concatenate(
        [
            ref[at][:, step * depth : (step + 1) * depth]
            for at in range(8)
            for ref in (own, other)
            for step in range(STEPS)
        ],
        axis=0,
    )
    count = STEPS * rows
    differs = core ^ at_y
    tile = 256
    for start in range(0, weight.shape[1], tile):
        part = jnp.dot(lhs, weight[:, start : start + tile], preferred_element_type=jnp.float32)
        part = part.astype(jnp.bfloat16)
        for at in range(8):
            distance = lax.rem(at - at_z + 8, 8)
            for side in range(2):
                first = (2 * at + side) * count
                terms[distance, differs ^ side, :, start : start + tile] = part[
                    first : first + count
                ]


def hop_dp(array, target):
    return lax.ppermute(array, "dp", [(s, target(s)) for s in range(16)])


def hop_tensor(array, target):
    return lax.ppermute(array, "tensor", [(s, target(s)) for s in range(16)])


def other_core(array):
    return hop_dp(array, lambda s: s ^ 1)


def other_half(array):
    return hop_dp(array, lambda s: s ^ 2)


def x_up(array):
    return hop_dp(array, lambda s: (s + 4) % 16)


def x_down(array):
    return hop_dp(array, lambda s: (s - 4) % 16)


def x_far(array):
    return hop_dp(array, lambda s: (s + 8) % 16)


def other_y(array):
    return hop_tensor(array, lambda s: s ^ 1)


def z_up(array):
    return hop_tensor(array, lambda s: (s + 2) % 16)


def z_down(array):
    return hop_tensor(array, lambda s: (s - 2) % 16)


def between_chips(array):
    groups = [[core + 2 * chip for chip in range(8)] for core in range(2)]
    return lax.all_to_all(array, "dp", 0, 0, axis_index_groups=groups)


def pick(array, index, axis=0):
    return lax.dynamic_index_in_dim(array, index, axis, keepdims=False)


def add_up(*arrays):
    total = arrays[0].astype(jnp.float32)
    for array in arrays[1:]:
        total = total + array.astype(jnp.float32)
    return total


def cores_summed(kept, sent):
    return add_up(kept, other_core(sent)).astype(kept.dtype)


def scatter_xy(block, half):
    kind = block(0).dtype
    far, ahead, behind = block(2), block(1), block(3)
    low, high = x_up(far[0]), x_down(far[1])
    ahead = jnp.stack([add_up(ahead[0], low).astype(kind), ahead[1]])
    behind = jnp.stack([behind[0], add_up(behind[1], high).astype(kind)])
    total = add_up(block(0), x_up(ahead), x_down(behind))
    kept, sent = pick(total, half), pick(total, 1 - half).astype(kind)
    return kept, other_half(sent)


def in_order(own, other, position):
    first = jnp.where(position == 0, own, other)
    second = jnp.where(position == 0, other, own)
    return first, second


def on_device(
    decoder_input,
    norm_multiplier,
    query_weight,
    key_weight,
    value_weight,
    output_weight,
    key_value_cache,
    lengths,
    training_input,
    query_gradient,
    attention_mixed,
    output_gradient,
    rewards,
    adapter_down,
    adapter_up,
    down_mean_moment,
    up_mean_moment,
    down_variance_moment,
    up_variance_moment,
):
    adapter_factor = 1.0 / math.sqrt(MODEL_WIDTH * FACTOR_RANK)
    dp_index = lax.axis_index("dp")
    tensor_index = lax.axis_index("tensor")
    at_x, half, core = dp_index // 4, (dp_index // 2) % 2, dp_index % 2
    at_z, at_y = tensor_index // 2, tensor_index % 2
    core_differs = core ^ at_y
    bf16 = jnp.bfloat16

    gain = norm_multiplier.astype(jnp.float32)[None, :]
    raw = decoder_input.reshape(STEPS * decoder_input.shape[1], -1)
    rows = (raw.astype(jnp.float32) * gain).astype(bf16)
    count = rows.shape[0]
    swap = [(i * 16 + j, j * 16 + i) for i in range(16) for j in range(16)]
    raw = jnp.concatenate([raw, jnp.broadcast_to(norm_multiplier[None, :], (16, raw.shape[1]))])
    turned_rows = lax.ppermute(raw, ("dp", "tensor"), swap)
    own = jnp.stack(in_order(rows, other_y(rows), core_differs))
    gathered = [own]
    up, down = own, own
    for _ in range(3):
        up, down = z_up(up), z_down(down)
        gathered += [up, down]
    gathered.append(jnp.stack([z_up(up[0]), z_down(down[1])]))

    def slot_of(distance):
        return jnp.where(distance < 4, 2 * distance, 15 - 2 * distance)

    tokens, width = training_input.shape
    rank = FACTOR_RANK
    ranks, query_cotangent, output_cotangent = call(
        rank_kernel,
        (shape((tokens, 4 * rank), bf16), shape((tokens, width), bf16), shape((tokens, width), bf16)),
        (
            rewards,
            training_input,
            query_gradient,
            attention_mixed,
            output_gradient,
            adapter_down,
            adapter_up,
        ),
        in_specs=[SMEM] + [ANY] * 6,
        flops=8 * tokens * width * rank,
        scratch=[pltpu.VMEM((tokens, width), bf16)] * 4
        + [pltpu.VMEM((2, rank, width), jnp.float32)] * 2
        + [pltpu.SemaphoreType.DMA((6,))],
        vmem=56,
    )
    others = [hop_tensor(ranks, lambda s, b=b: s ^ b) for b in (1, 2, 3)]
    ranks = add_up(ranks, *others).astype(bf16)
    others = [hop_tensor(ranks, lambda s, b=b: s ^ b) for b in (4, 8, 12)]
    kept, sent = call(
        gradient_kernel,
        (shape((8, 16, width), bf16), shape((8, 16, width), bf16)),
        (
            ranks,
            *others,
            training_input,
            attention_mixed,
            query_cotangent,
            output_cotangent,
            *gathered[1:3],
        ),
        in_specs=[VMEM] * 8 + [ANY] * 2,
        flops=8 * tokens * width * rank,
    )
    block = (2, 16, width)
    near, ahead, far, behind = call(
        spread_kernel,
        (shape(block, jnp.float32), *[shape(block, bf16)] * 3),
        (kept, other_core(sent), *gathered[3:5]),
        in_specs=[VMEM] * 2 + [ANY] * 2,
    )
    (total,) = call(
        lambda *refs: sum_kernel(4, *refs),
        (shape(block, bf16),),
        (near, x_up(ahead), x_far(far), x_down(behind), *gathered[5:7]),
        in_specs=[VMEM] * 4 + [ANY] * 2,
    )
    (total,) = call(
        lambda *refs: sum_kernel(2, *refs),
        (shape(block, bf16),),
        (total, other_half(total), gathered[7]),
        in_specs=[VMEM] * 2 + [ANY],
    )
    around = jnp.stack([total, x_down(total), x_far(total), x_up(total)])

    head_cols = query_weight.shape[1]
    kv_cols = key_weight.shape[1]
    sums = []
    for first, last in ((0, 3), (3, 5), (5, 8)):
        number = last - first
        cols = head_cols + 2 * kv_cols
        kept, sent = call(
            lambda *refs, number=number: project_kernel(number, *refs),
            (shape((number, count, cols), bf16), shape((number, count, cols), bf16)),
            (*gathered[first:last], query_weight, key_weight.T, value_weight.T),
            flops=4 * number * count * width * cols,
        )
        sums.append(cores_summed(kept, sent))
    adam = call(
        adam_kernel,
        (
            *[shape(adapter_down.shape, jnp.float32)] * 2,
            *[shape(adapter_down.shape, bf16)] * 4,
            *[shape((rank, width), bf16)] * 4,
            shape((count, 2 * rank), jnp.float32),
        ),
        (
            around,
            other_core(around),
            turned_rows,
            adapter_down,
            adapter_up,
            down_mean_moment,
            up_mean_moment,
            down_variance_moment,
            up_variance_moment,
            kept,
        ),
        in_specs=[VMEM] * 9 + [ANY],
        flops=2 * count * width * 2 * rank,
    )
    refreshed_down, refreshed_up = adam[:2]
    refreshed_down_mean, refreshed_up_mean = adam[2:4]
    refreshed_down_variance, refreshed_up_variance = adam[4:6]
    down_one, up_zero, up_one, extra = adam[7:]
    up_block = lax.ppermute(up_one, ("dp", "tensor"), swap)
    others = [hop_tensor(extra, lambda s, b=b: s ^ b) for b in (1, 2, 3)]
    extra = add_up(extra, *others)
    others = [hop_tensor(extra, lambda s, b=b: s ^ b) for b in (4, 8, 12)]
    sums = jnp.concatenate(sums)

    def for_x(blocks):
        def block(d):
            first = (2 * ((at_x + d) % 4) - at_z) % 8
            return jnp.stack([pick(blocks, slot_of(first)), pick(blocks, slot_of((first + 1) % 8))])

        return block

    kept, received = scatter_xy(for_x(sums), half)
    local_row = key_value_cache.shape[0]
    step_rows = count // STEPS
    (mine,) = call(
        join_kernel,
        (shape((step_rows, STEPS * (head_cols + 2 * kv_cols)), bf16),),
        (kept, received, extra, *others, up_zero, up_block),
        in_specs=[VMEM] * 7 + [ANY],
    )
    mine = mine.reshape(16, local_row, -1)
    heads = lax.all_to_all(mine, "tensor", split_axis=0, concat_axis=0)
    heads = heads.reshape(16, local_row, STEPS, head_cols + 2 * kv_cols)
    queries = heads[..., :head_cols].reshape(
        KEY_VALUE_HEADS, 2, local_row, STEPS, head_cols // HEAD_WIDTH, HEAD_WIDTH
    )
    queries = queries.transpose(2, 0, 3, 1, 4, 5).reshape(
        local_row, KEY_VALUE_HEADS, STEPS * QUERY_HEADS // KEY_VALUE_HEADS, HEAD_WIDTH
    )
    fresh = heads[..., head_cols:].reshape(KEY_VALUE_HEADS, 2, local_row, STEPS, 2, kv_cols)
    fresh = fresh.transpose(4, 2, 3, 0, 1, 5).reshape(
        2, local_row, STEPS, KEY_VALUE_HEADS, HEAD_WIDTH
    )
    cache_of_keys = key_value_cache[:, :, 0, :].reshape(
        local_row, CACHE_SLOTS, KEY_VALUE_HEADS, HEAD_WIDTH
    )
    cache_of_values = key_value_cache[:, :, 1, :].reshape(
        local_row, CACHE_SLOTS, KEY_VALUE_HEADS, HEAD_WIDTH
    )
    valid = jnp.arange(CACHE_SLOTS, dtype=jnp.int32)[None, :] < lengths[:, None]
    attended = attend_rows(queries, cache_of_keys, cache_of_values, valid, fresh[0], fresh[1])
    attended = attended.reshape(
        local_row, KEY_VALUE_HEADS, STEPS, 2, head_cols // HEAD_WIDTH, HEAD_WIDTH
    )
    attended = attended.transpose(1, 3, 0, 2, 4, 5).reshape(16, local_row, STEPS * head_cols)
    head_block = lax.all_to_all(attended, "tensor", split_axis=0, concat_axis=0)
    head_block = head_block.reshape(step_rows, STEPS * head_cols)
    output_combined = (
        output_weight.astype(jnp.float32)
        + adapter_factor * leading_contraction(down_one, up_block)
    ).astype(bf16)
    around = between_chips(jnp.broadcast_to(head_block[None], (8, *head_block.shape)))
    out_cols = output_weight.shape[1]
    (terms,) = call(
        output_kernel,
        (shape((8, 2, count, out_cols), bf16),),
        (around, other_core(around), output_combined),
        flops=32 * count * head_cols * out_cols,
        vmem=32,
    )
    low, high = z_up(terms[4, 0]), z_down(terms[4, 1])
    up = jnp.stack([add_up(terms[3, 0], low).astype(bf16), terms[3, 1]])
    down = jnp.stack([terms[5, 0], add_up(terms[5, 1], high).astype(bf16)])
    for d in (2, 1):
        up = add_up(terms[d], z_up(up)).astype(bf16)
        down = add_up(terms[8 - d], z_down(down)).astype(bf16)
    total = add_up(terms[0], z_up(up), z_down(down))
    attn_out = add_up(total[0], other_y(total[1].astype(bf16))).astype(bf16)
    return (
        attn_out.reshape(STEPS, step_rows, out_cols),
        refreshed_down,
        refreshed_up,
        refreshed_down_mean,
        refreshed_up_mean,
        refreshed_down_variance,
        refreshed_up_variance,
    )


def solution(mesh):
    in_specs = (
        P(None, "tensor", "dp"),
        P("dp"),
        P("dp", "tensor"),
        P("dp", "tensor"),
        P("dp", "tensor"),
        P("tensor", "dp"),
        P(("dp", "tensor"), None, None, None),
        P(("dp", "tensor")),
        P("dp", "tensor"),
        P("dp", "tensor"),
        P("dp", "tensor"),
        P("dp", "tensor"),
        P(),
        P(None, None, "tensor"),
        P(None, None, "tensor"),
        P(None, None, "tensor"),
        P(None, None, "tensor"),
        P(None, None, "tensor"),
        P(None, None, "tensor"),
    )
    out_specs = (
        P(None, "tensor", "dp"),
        P(None, None, "tensor"),
        P(None, None, "tensor"),
        P(None, None, "tensor"),
        P(None, None, "tensor"),
        P(None, None, "tensor"),
        P(None, None, "tensor"),
    )
    return jax.shard_map(
        on_device, mesh=mesh, in_specs=in_specs, out_specs=out_specs, check_vma=False
    )
```

```python
import math

import jax
import jax.numpy as jnp
from jax import lax
from jax.experimental import pallas as pl
from jax.experimental.pallas import tpu as pltpu
from jax.sharding import PartitionSpec as P

MODEL_WIDTH = 16384
QUERY_HEADS = 128
HEAD_WIDTH = 128
KEY_VALUE_HEADS = 8
FACTOR_RANK = 64
STEPS = 2
CACHE_SLOTS = 128
SEQLEN = 64
GROUP = 8


BETA_ONE = 0.9
BETA_TWO = 0.999
BIAS_ONE = 0.271
BIAS_TWO = 0.002997001
LEARN_RATE = 0.3
ADAM_EPS = 1e-08
NORM_EPS = 1e-05
NEG_FILL = -1e30


def apply_adam_rule(parameter, gradient, first_moment, second_moment):
    moment_one = BETA_ONE * first_moment.astype(jnp.float32) + (1.0 - BETA_ONE) * gradient
    moment_two = (
        BETA_TWO * second_moment.astype(jnp.float32) + (1.0 - BETA_TWO) * gradient * gradient
    )
    change = moment_one / BIAS_ONE / (jnp.sqrt(moment_two / BIAS_TWO) + ADAM_EPS)
    return (
        parameter - LEARN_RATE * change,
        moment_one.astype(jnp.bfloat16),
        moment_two.astype(jnp.bfloat16),
    )


def leading_contraction(lhs_array, rhs_array):
    return lax.dot_general(
        lhs_array, rhs_array, (((0,), (0,)), ((), ())), preferred_element_type=jnp.float32
    )


def contract_last(lhs_array, rhs_array):
    return lax.dot_general(
        lhs_array, rhs_array, (((1,), (1,)), ((), ())), preferred_element_type=jnp.float32
    )


def attend_rows(query_rows, cache_of_keys, cache_of_values, valid, latest_keys, latest_values):
    scale_att = 1.0 / math.sqrt(HEAD_WIDTH)
    cache_scores = (
        jnp.einsum("rkgd,rpkd->rkgp", query_rows, cache_of_keys, preferred_element_type=jnp.float32)
        * scale_att
    )
    cache_scores = jnp.where(valid[:, None, None, :], cache_scores, NEG_FILL)
    fresh_scores = (
        jnp.einsum("rkgd,rpkd->rkgp", query_rows, latest_keys, preferred_element_type=jnp.float32)
        * scale_att
    )
    group = QUERY_HEADS // KEY_VALUE_HEADS
    query_step = jnp.arange(STEPS * group, dtype=jnp.int32) // group
    seen = jnp.arange(STEPS, dtype=jnp.int32)[None, :] <= query_step[:, None]
    fresh_scores = jnp.where(seen[None, None], fresh_scores, NEG_FILL)
    scores = jnp.concatenate([cache_scores, fresh_scores], axis=-1)
    row_top = jnp.max(scores, axis=-1, keepdims=True)
    exponent = jnp.exp(scores - row_top)
    attention_weights = (exponent / jnp.sum(exponent, axis=-1, keepdims=True)).astype(jnp.bfloat16)
    cache_part = jnp.einsum(
        "rkgp,rpkd->rkgd",
        attention_weights[..., :CACHE_SLOTS],
        cache_of_values,
        preferred_element_type=jnp.float32,
    )
    fresh_part = jnp.einsum(
        "rkgp,rpkd->rkgd",
        attention_weights[..., CACHE_SLOTS:],
        latest_values,
        preferred_element_type=jnp.float32,
    )
    return (cache_part + fresh_part).astype(jnp.bfloat16)


VMEM = pl.BlockSpec(memory_space=pltpu.VMEM)
SMEM = pl.BlockSpec(memory_space=pltpu.SMEM)
ANY = pl.BlockSpec(memory_space=pl.ANY)


def call(kernel, out_shape, inputs, in_specs=None, flops=0, scratch=(), vmem=10):
    moved = sum(a.size * a.dtype.itemsize for a in (*inputs, *out_shape))
    return pl.pallas_call(
        kernel,
        out_shape=out_shape,
        in_specs=in_specs or [VMEM] * len(inputs),
        out_specs=[VMEM] * len(out_shape),
        scratch_shapes=list(scratch),
        compiler_params=pltpu.CompilerParams(vmem_limit_bytes=vmem * 2**20),
        cost_estimate=pl.CostEstimate(flops=flops, bytes_accessed=moved, transcendentals=0),
    )(*inputs)


def shape(dims, kind):
    return jax.ShapeDtypeStruct(dims, kind)


def rank_kernel(rewards, gain, *refs):
    sources, (scaled, ranks, query_cot, out_cot), copies = refs[:7], refs[7:11], refs[11:18]
    started = [
        pltpu.make_async_copy(source, copy, refs[18].at[number])
        for number, (source, copy) in enumerate(zip(sources, copies))
    ]
    for copy in started:
        copy.start()
    for copy in started:
        copy.wait()
    rows, inputs, query_grad, mixed, out_grad, down, up = copies
    multiplier = gain[...].astype(jnp.float32).reshape(1, -1)
    for step in range(STEPS):
        span = slice(step * rows.shape[1], (step + 1) * rows.shape[1])
        scaled[span] = (rows[step].astype(jnp.float32) * multiplier).astype(jnp.bfloat16)
    tokens = inputs.shape[0]
    first = lax.axis_index("dp") * (tokens // SEQLEN)
    group = (first // GROUP) * GROUP
    total = rewards[group]
    for member in range(1, GROUP):
        total = total + rewards[group + member]
    mean = total.astype(jnp.float32) * (1.0 / GROUP)
    for seq in range(tokens // SEQLEN):
        weight = rewards[first + seq].astype(jnp.float32) - mean
        span = slice(seq * SEQLEN, (seq + 1) * SEQLEN)
        query_cot[span, :] = (weight * query_grad[span, :].astype(jnp.float32)).astype(jnp.bfloat16)
        out_cot[span, :] = (weight * out_grad[span, :].astype(jnp.float32)).astype(jnp.bfloat16)
    ranks[...] = jnp.concatenate(
        [
            contract_last(inputs[...], down[0].astype(jnp.bfloat16)),
            contract_last(mixed[...], down[1].astype(jnp.bfloat16)),
            contract_last(query_cot[...], up[0].astype(jnp.bfloat16)),
            contract_last(out_cot[...], up[1].astype(jnp.bfloat16)),
        ],
        axis=1,
    ).astype(jnp.bfloat16)


def gradient_kernel(own, one, two, three, inputs, mixed, query_cot, out_cot, *refs):
    keep, send = refs[-2:]
    ranks = add_up(own[...], one[...], two[...], three[...])
    turned = ranks.T.astype(jnp.bfloat16)
    rank = FACTOR_RANK
    core = lax.axis_index("dp") % 2
    order = ((2, inputs), (3, mixed), (0, query_cot), (1, out_cot))
    for place, (which, other) in enumerate(order):
        part = jnp.dot(
            turned[which * rank : (which + 1) * rank],
            other[...],
            preferred_element_type=jnp.float32,
        ).astype(jnp.bfloat16)
        for block in range(rank // 32):
            even = part[block * 32 : block * 32 + 16]
            odd = part[block * 32 + 16 : block * 32 + 32]
            at = place * (rank // 32) + block
            keep[at] = jnp.where(core == 0, even, odd)
            send[at] = jnp.where(core == 0, odd, even)


def project_kernel(count, *refs):
    blocks, (query, key_turned, value_turned) = refs[:count], refs[count : count + 3]
    keep, send = refs[-2:]
    rows = blocks[0].shape[1]
    head_cols, kv_cols = query.shape[1], key_turned.shape[0]
    lhs = jnp.concatenate([b[side] for side in (0, 1) for b in blocks], axis=0)
    tile = 256

    def store(result, start, stop):
        result = result.astype(jnp.bfloat16)
        for at in range(count):
            keep[at, :, start:stop] = result[at * rows : (at + 1) * rows]
            other = (count + at) * rows
            send[at, :, start:stop] = result[other : other + rows]

    for start in range(0, head_cols, tile):
        part = jnp.dot(lhs, query[:, start : start + tile], preferred_element_type=jnp.float32)
        store(part, start, start + tile)
    turned = jnp.concatenate([key_turned[...], value_turned[...]], axis=0)
    store(contract_last(lhs, turned), head_cols, head_cols + 2 * kv_cols)


def spread_kernel(kept, received, *refs):
    at_x = lax.axis_index("dp") // 4
    for distance, out in enumerate(refs[-4:]):
        x = lax.rem(at_x + distance, 4)
        for half in range(2):
            out[half] = add_up(kept[2 * x + half], received[2 * x + half]).astype(out.dtype)


def sum_kernel(count, *refs):
    refs[-1][...] = add_up(*[ref[...] for ref in refs[:count]]).astype(refs[-1].dtype)


def pair_kernel(own, other, _, out):
    differs = (lax.axis_index("dp") % 2) ^ (lax.axis_index("tensor") % 2)
    mine, theirs = own[...], other[...]
    out[0] = jnp.where(differs == 0, mine, theirs)
    out[1] = jnp.where(differs == 0, theirs, mine)


def raw_kernel(rows, gain, _, out):
    count = STEPS * rows.shape[1]
    for step in range(STEPS):
        out[step * rows.shape[1] : (step + 1) * rows.shape[1]] = rows[step]
    multiplier = gain[...].astype(jnp.float32).reshape(1, -1)
    out[count:] = jnp.broadcast_to(multiplier, (16, out.shape[1])).astype(out.dtype)


def halves_kernel(up, down, _, first, second):
    first[...] = up[0]
    second[...] = down[1]


def join_kernel(kept, received, own, one, two, three, up_zero, _, out):
    rank = up_zero.shape[0]
    extra = add_up(own[...], one[...], two[...], three[...])
    inverse = lax.rsqrt(extra[:, rank : rank + 1] / MODEL_WIDTH + NORM_EPS)
    low_rank = extra[:, :rank].astype(jnp.bfloat16)
    adapter_factor = 1.0 / math.sqrt(MODEL_WIDTH * FACTOR_RANK)
    head_cols, cols = up_zero.shape[1], kept.shape[1]
    step_rows = out.shape[0]
    change = adapter_factor * jnp.dot(
        low_rank, up_zero[...], preferred_element_type=jnp.float32
    )
    base = add_up(kept[...], received[...])
    for start, stop, value in (
        (0, head_cols, base[:, :head_cols] + change),
        (head_cols, cols, base[:, head_cols:]),
    ):
        value = jnp.where(inverse > 0.0, value * inverse, 0.0).astype(jnp.bfloat16)
        for step in range(STEPS):
            out[:, step * cols + start : step * cols + stop] = value[
                step * step_rows : (step + 1) * step_rows
            ]


def adam_kernel(own, other, rows, *refs):
    (down, up, down_mean, up_mean, down_var, up_var), outs = refs[:6], refs[-11:]
    new_down, new_up, new_down_mean, new_up_mean, new_down_var, new_up_var = outs[:6]
    down_zero, down_one, up_zero, up_one, products = outs[6:]
    dp = lax.axis_index("dp")
    at_x, core = dp // 4, dp % 2
    adapter_factor = 1.0 / math.sqrt(MODEL_WIDTH * FACTOR_RANK)
    old = ((down, down_mean, down_var), (up, up_mean, up_var))
    new = ((new_down, new_down_mean, new_down_var), (new_up, new_up_mean, new_up_var))
    low = ((down_zero, down_one), (up_zero, up_one))
    for factor in range(4):
        side, which = factor // 2, factor % 2
        distance = lax.rem(factor - at_x + 4, 4)
        for half in range(2):
            mine, theirs = own[distance, half], other[distance, half]
            pair = (jnp.where(core == 0, mine, theirs), jnp.where(core == 0, theirs, mine))
            for number in range(2):
                at = (half * 2 + number) * 16
                span = slice(at, at + 16)
                gradient = adapter_factor * pair[number].astype(jnp.float32)
                result = apply_adam_rule(
                    old[side][0][which, span],
                    gradient,
                    old[side][1][which, span],
                    old[side][2][which, span],
                )
                for target, value in zip(new[side], result):
                    target[which, span] = value
                low[side][which][span] = result[0].astype(jnp.bfloat16)
    count = products.shape[0]
    rank = down_zero.shape[0]
    raw = rows[:count].astype(jnp.float32)
    scaled = (raw * rows[count : count + 1].astype(jnp.float32)).astype(jnp.bfloat16)
    factor = down_zero[...]
    product = contract_last(scaled, jnp.concatenate([factor, jnp.zeros_like(factor)], axis=0))
    squares = jnp.sum(raw * raw, axis=1, keepdims=True)
    lane = lax.broadcasted_iota(jnp.int32, product.shape, 1)
    products[...] = jnp.where(lane < rank, product, squares)


def output_kernel(own, other, weight, terms):
    rows, depth = own.shape[1], weight.shape[0]
    at_z, at_y = lax.axis_index("tensor") // 2, lax.axis_index("tensor") % 2
    core = lax.axis_index("dp") % 2
    lhs = jnp.concatenate(
        [
            ref[at][:, step * depth : (step + 1) * depth]
            for at in range(8)
            for ref in (own, other)
            for step in range(STEPS)
        ],
        axis=0,
    )
    count = STEPS * rows
    differs = core ^ at_y
    tile = 256
    for start in range(0, weight.shape[1], tile):
        part = jnp.dot(lhs, weight[:, start : start + tile], preferred_element_type=jnp.float32)
        part = part.astype(jnp.bfloat16)
        for at in range(8):
            distance = lax.rem(at - at_z + 8, 8)
            for side in range(2):
                first = (2 * at + side) * count
                terms[distance, differs ^ side, :, start : start + tile] = part[
                    first : first + count
                ]


def hop_dp(array, target):
    return lax.ppermute(array, "dp", [(s, target(s)) for s in range(16)])


def hop_tensor(array, target):
    return lax.ppermute(array, "tensor", [(s, target(s)) for s in range(16)])


def other_core(array):
    return hop_dp(array, lambda s: s ^ 1)


def other_half(array):
    return hop_dp(array, lambda s: s ^ 2)


def x_up(array):
    return hop_dp(array, lambda s: (s + 4) % 16)


def x_down(array):
    return hop_dp(array, lambda s: (s - 4) % 16)


def x_far(array):
    return hop_dp(array, lambda s: (s + 8) % 16)


def other_y(array):
    return hop_tensor(array, lambda s: s ^ 1)


def z_up(array):
    return hop_tensor(array, lambda s: (s + 2) % 16)


def z_down(array):
    return hop_tensor(array, lambda s: (s - 2) % 16)


def between_chips(array):
    groups = [[core + 2 * chip for chip in range(8)] for core in range(2)]
    return lax.all_to_all(array, "dp", 0, 0, axis_index_groups=groups)


def pick(array, index, axis=0):
    return lax.dynamic_index_in_dim(array, index, axis, keepdims=False)


def add_up(*arrays):
    total = arrays[0].astype(jnp.float32)
    for array in arrays[1:]:
        total = total + array.astype(jnp.float32)
    return total


def cores_summed(kept, sent):
    return add_up(kept, other_core(sent)).astype(kept.dtype)


def scatter_xy(block, half):
    kind = block(0).dtype
    far, ahead, behind = block(2), block(1), block(3)
    low, high = x_up(far[0]), x_down(far[1])
    ahead = jnp.stack([add_up(ahead[0], low).astype(kind), ahead[1]])
    behind = jnp.stack([behind[0], add_up(behind[1], high).astype(kind)])
    total = add_up(block(0), x_up(ahead), x_down(behind))
    kept, sent = pick(total, half), pick(total, 1 - half).astype(kind)
    return kept, other_half(sent)


def in_order(own, other, position):
    first = jnp.where(position == 0, own, other)
    second = jnp.where(position == 0, other, own)
    return first, second


def on_device(
    decoder_input,
    norm_multiplier,
    query_weight,
    key_weight,
    value_weight,
    output_weight,
    key_value_cache,
    lengths,
    training_input,
    query_gradient,
    attention_mixed,
    output_gradient,
    rewards,
    adapter_down,
    adapter_up,
    down_mean_moment,
    up_mean_moment,
    down_variance_moment,
    up_variance_moment,
):
    adapter_factor = 1.0 / math.sqrt(MODEL_WIDTH * FACTOR_RANK)
    dp_index = lax.axis_index("dp")
    tensor_index = lax.axis_index("tensor")
    at_x, half, core = dp_index // 4, (dp_index // 2) % 2, dp_index % 2
    at_z, at_y = tensor_index // 2, tensor_index % 2
    core_differs = core ^ at_y
    bf16 = jnp.bfloat16

    count = STEPS * decoder_input.shape[1]
    tokens, width = training_input.shape
    rank = FACTOR_RANK
    rows, ranks, query_cotangent, output_cotangent = call(
        rank_kernel,
        (
            shape((count, width), bf16),
            shape((tokens, 4 * rank), bf16),
            shape((tokens, width), bf16),
            shape((tokens, width), bf16),
        ),
        (
            rewards,
            norm_multiplier,
            decoder_input,
            training_input,
            query_gradient,
            attention_mixed,
            output_gradient,
            adapter_down,
            adapter_up,
        ),
        in_specs=[SMEM, VMEM] + [ANY] * 7,
        flops=8 * tokens * width * rank,
        scratch=[pltpu.VMEM(decoder_input.shape, bf16)]
        + [pltpu.VMEM((tokens, width), bf16)] * 4
        + [pltpu.VMEM((2, rank, width), jnp.float32)] * 2
        + [pltpu.SemaphoreType.DMA((7,))],
        vmem=56,
    )
    def slot_of(distance):
        return jnp.where(distance < 4, 2 * distance, 15 - 2 * distance)

    others = [hop_tensor(ranks, lambda s, b=b: s ^ b) for b in (1, 2, 3)]
    ranks = add_up(ranks, *others).astype(bf16)
    (own,) = call(
        pair_kernel,
        (shape((2, count, width), bf16),),
        (rows, other_y(rows), ranks),
        in_specs=[VMEM, VMEM, ANY],
    )
    gathered = [own]
    up, down = own, own
    for _ in range(3):
        up, down = z_up(up), z_down(down)
        gathered += [up, down]
    others = [hop_tensor(ranks, lambda s, b=b: s ^ b) for b in (4, 8, 12)]
    kept, sent = call(
        gradient_kernel,
        (shape((8, 16, width), bf16), shape((8, 16, width), bf16)),
        (
            ranks,
            *others,
            training_input,
            attention_mixed,
            query_cotangent,
            output_cotangent,
            *gathered[1:3],
        ),
        in_specs=[VMEM] * 8 + [ANY] * 2,
        flops=8 * tokens * width * rank,
    )
    block = (2, 16, width)
    near, ahead, far, behind = call(
        spread_kernel,
        (shape(block, jnp.float32), *[shape(block, bf16)] * 3),
        (kept, other_core(sent), *gathered[3:5]),
        in_specs=[VMEM] * 2 + [ANY] * 2,
    )
    (total,) = call(
        lambda *refs: sum_kernel(4, *refs),
        (shape(block, bf16),),
        (near, x_up(ahead), x_far(far), x_down(behind), *gathered[5:7]),
        in_specs=[VMEM] * 4 + [ANY] * 2,
    )
    swap = [(i * 16 + j, j * 16 + i) for i in range(16) for j in range(16)]
    (raw,) = call(
        raw_kernel,
        (shape((count + 16, width), bf16),),
        (decoder_input, norm_multiplier, total),
        in_specs=[VMEM, VMEM, ANY],
    )
    turned_rows = lax.ppermute(raw, ("dp", "tensor"), swap)
    first, second = call(
        halves_kernel,
        [shape((count, width), bf16)] * 2,
        (up, down, total),
        in_specs=[VMEM, VMEM, ANY],
    )
    gathered.append(jnp.stack([z_up(first), z_down(second)]))
    (total,) = call(
        lambda *refs: sum_kernel(2, *refs),
        (shape(block, bf16),),
        (total, other_half(total), gathered[7]),
        in_specs=[VMEM] * 2 + [ANY],
    )
    around = jnp.stack([total, x_down(total), x_far(total), x_up(total)])
    head_cols = query_weight.shape[1]
    kv_cols = key_weight.shape[1]
    sums = []
    for first, last in ((0, 3), (3, 5), (5, 8)):
        number = last - first
        cols = head_cols + 2 * kv_cols
        kept, sent = call(
            lambda *refs, number=number: project_kernel(number, *refs),
            (shape((number, count, cols), bf16), shape((number, count, cols), bf16)),
            (*gathered[first:last], query_weight, key_weight.T, value_weight.T),
            flops=4 * number * count * width * cols,
        )
        sums.append(cores_summed(kept, sent))
    adam = call(
        adam_kernel,
        (
            *[shape(adapter_down.shape, jnp.float32)] * 2,
            *[shape(adapter_down.shape, bf16)] * 4,
            *[shape((rank, width), bf16)] * 4,
            shape((count, 2 * rank), jnp.float32),
        ),
        (
            around,
            other_core(around),
            turned_rows,
            adapter_down,
            adapter_up,
            down_mean_moment,
            up_mean_moment,
            down_variance_moment,
            up_variance_moment,
            kept,
        ),
        in_specs=[VMEM] * 9 + [ANY],
        flops=2 * count * width * 2 * rank,
    )
    refreshed_down, refreshed_up = adam[:2]
    refreshed_down_mean, refreshed_up_mean = adam[2:4]
    refreshed_down_variance, refreshed_up_variance = adam[4:6]
    down_one, up_zero, up_one, extra = adam[7:]
    up_block = lax.ppermute(up_one, ("dp", "tensor"), swap)
    others = [hop_tensor(extra, lambda s, b=b: s ^ b) for b in (1, 2, 3)]
    extra = add_up(extra, *others)
    others = [hop_tensor(extra, lambda s, b=b: s ^ b) for b in (4, 8, 12)]
    sums = jnp.concatenate(sums)

    def for_x(blocks):
        def block(d):
            first = (2 * ((at_x + d) % 4) - at_z) % 8
            return jnp.stack([pick(blocks, slot_of(first)), pick(blocks, slot_of((first + 1) % 8))])

        return block

    kept, received = scatter_xy(for_x(sums), half)
    local_row = key_value_cache.shape[0]
    step_rows = count // STEPS
    (mine,) = call(
        join_kernel,
        (shape((step_rows, STEPS * (head_cols + 2 * kv_cols)), bf16),),
        (kept, received, extra, *others, up_zero, up_block),
        in_specs=[VMEM] * 7 + [ANY],
    )
    mine = mine.reshape(16, local_row, -1)
    heads = lax.all_to_all(mine, "tensor", split_axis=0, concat_axis=0)
    heads = heads.reshape(16, local_row, STEPS, head_cols + 2 * kv_cols)
    queries = heads[..., :head_cols].reshape(
        KEY_VALUE_HEADS, 2, local_row, STEPS, head_cols // HEAD_WIDTH, HEAD_WIDTH
    )
    queries = queries.transpose(2, 0, 3, 1, 4, 5).reshape(
        local_row, KEY_VALUE_HEADS, STEPS * QUERY_HEADS // KEY_VALUE_HEADS, HEAD_WIDTH
    )
    fresh = heads[..., head_cols:].reshape(KEY_VALUE_HEADS, 2, local_row, STEPS, 2, kv_cols)
    fresh = fresh.transpose(4, 2, 3, 0, 1, 5).reshape(
        2, local_row, STEPS, KEY_VALUE_HEADS, HEAD_WIDTH
    )
    cache_of_keys = key_value_cache[:, :, 0, :].reshape(
        local_row, CACHE_SLOTS, KEY_VALUE_HEADS, HEAD_WIDTH
    )
    cache_of_values = key_value_cache[:, :, 1, :].reshape(
        local_row, CACHE_SLOTS, KEY_VALUE_HEADS, HEAD_WIDTH
    )
    valid = jnp.arange(CACHE_SLOTS, dtype=jnp.int32)[None, :] < lengths[:, None]
    attended = attend_rows(queries, cache_of_keys, cache_of_values, valid, fresh[0], fresh[1])
    attended = attended.reshape(
        local_row, KEY_VALUE_HEADS, STEPS, 2, head_cols // HEAD_WIDTH, HEAD_WIDTH
    )
    attended = attended.transpose(1, 3, 0, 2, 4, 5).reshape(16, local_row, STEPS * head_cols)
    head_block = lax.all_to_all(attended, "tensor", split_axis=0, concat_axis=0)
    head_block = head_block.reshape(step_rows, STEPS * head_cols)
    output_combined = (
        output_weight.astype(jnp.float32)
        + adapter_factor * leading_contraction(down_one, up_block)
    ).astype(bf16)
    around = between_chips(jnp.broadcast_to(head_block[None], (8, *head_block.shape)))
    out_cols = output_weight.shape[1]
    (terms,) = call(
        output_kernel,
        (shape((8, 2, count, out_cols), bf16),),
        (around, other_core(around), output_combined),
        flops=32 * count * head_cols * out_cols,
        vmem=16,
    )
    low, high = z_up(terms[4, 0]), z_down(terms[4, 1])
    up = jnp.stack([add_up(terms[3, 0], low).astype(bf16), terms[3, 1]])
    down = jnp.stack([terms[5, 0], add_up(terms[5, 1], high).astype(bf16)])
    for d in (2, 1):
        up = add_up(terms[d], z_up(up)).astype(bf16)
        down = add_up(terms[8 - d], z_down(down)).astype(bf16)
    total = add_up(terms[0], z_up(up), z_down(down))
    attn_out = add_up(total[0], other_y(total[1].astype(bf16))).astype(bf16)
    return (
        attn_out.reshape(STEPS, step_rows, out_cols),
        refreshed_down,
        refreshed_up,
        refreshed_down_mean,
        refreshed_up_mean,
        refreshed_down_variance,
        refreshed_up_variance,
    )


def solution(mesh):
    in_specs = (
        P(None, "tensor", "dp"),
        P("dp"),
        P("dp", "tensor"),
        P("dp", "tensor"),
        P("dp", "tensor"),
        P("tensor", "dp"),
        P(("dp", "tensor"), None, None, None),
        P(("dp", "tensor")),
        P("dp", "tensor"),
        P("dp", "tensor"),
        P("dp", "tensor"),
        P("dp", "tensor"),
        P(),
        P(None, None, "tensor"),
        P(None, None, "tensor"),
        P(None, None, "tensor"),
        P(None, None, "tensor"),
        P(None, None, "tensor"),
        P(None, None, "tensor"),
    )
    out_specs = (
        P(None, "tensor", "dp"),
        P(None, None, "tensor"),
        P(None, None, "tensor"),
        P(None, None, "tensor"),
        P(None, None, "tensor"),
        P(None, None, "tensor"),
        P(None, None, "tensor"),
    )
    return jax.shard_map(
        on_device, mesh=mesh, in_specs=in_specs, out_specs=out_specs, check_vma=False
    )
```
